32 devices in a mesh: dom: 32 (over z, y, x, core).
Axes of the slice: x: 2, y: 2, z: 4, core: 2. Of those that a mesh axis runs over, the one named last changes fastest.
Arguments:
- features: bfloat16 [65536, 512], P('dom'), may hold values from -6 to 6
- weight: bfloat16 [512, 512], replicated, may hold values from -0.25 to 0.25
- cotangent: bfloat16 [65536, 512], P('dom'), may hold values from -6 to 6
- tile_values: bfloat16 [3072, 128, 128], P('dom'), may hold values from -0.21875 to 0.21875
- tile_rows: int32 [3072], P('dom'), may hold values from 0 to 15
- tile_cols: int32 [3072], P('dom'), may hold values from 0 to 18, as said below
- hub_rows: int32 [128], P('dom'), may hold values from 0 to 2047
- send_rows: int32 [32, 32, 8], P('dom'), may hold values from 0 to 2047
- send_count: int32 [32, 32], P('dom'), may hold values from 1 to 8, as said below
Outputs:
- output: bfloat16 [65536, 512], P('dom')
- grad_features: bfloat16 [65536, 512], P('dom')
- grad_weight: float32 [512, 512], replicated
The draws below stay inside these ranges and needn't reach their ends.
Inputs may be any that keep to these rules, and one draw needn't show every extreme that they name: `tile_cols`: on every device the first 64 tiles name column blocks below 17 and the other 32 name blocks from 17 on. `send_count`: every source sends 8 rows to at least one device.
All inputs are finite; a program needn't handle non-finite values.
Results may differ from the reference program's by a relative error of at most 0.019.
Values may be sent and summed in bfloat16 or wider, within the bound.
No kernel may reach another device: no remote copies, remote signals or barrier semaphores. Data moves between devices by JAX's collectives and lax.ppermute only.
A program may use at most 128 MiB of HBM per device.

```python
import jax
import jax.numpy as jnp
from jax import lax

F = 512
TILE = 128
R_DEV = 2048
LOC_TILES = 64
HALO_TILES = 32
HUBS_DEV = 4
SLOTS = 8
TILES_DEV = 96
VERTICES = 65536
TILES = 3072
HUBS = 128
ROW_BLOCKS = 16
LOC_BLOCKS = 17
EXT_BLOCKS = 19
N_DOM = 32


def draw_tile_cols(key, part):
    key_near, key_far, key_pick = jax.random.split(key, 3)
    near = jax.random.randint(key_near, (N_DOM, LOC_TILES), 0, LOC_BLOCKS)
    far = jax.random.randint(key_far, (N_DOM, HALO_TILES), LOC_BLOCKS, EXT_BLOCKS)
    chosen = jax.random.randint(key_pick, (), 0, N_DOM)
    near = near.at[chosen, 0].set(0)
    far = far.at[chosen, HALO_TILES - 1].set(EXT_BLOCKS - 1)
    return jnp.concatenate([near, far], axis=1).reshape(-1).astype(jnp.int32)


def draw_send_count(key, part):
    key_count, key_offset = jax.random.split(key, 2)
    counts = jax.random.randint(key_count, (N_DOM, N_DOM), 1, SLOTS + 1)
    offset = jax.random.randint(key_offset, (N_DOM,), 0, N_DOM)
    senders = jnp.arange(N_DOM, dtype=jnp.int32)
    filled = senders[None, :] == ((senders + offset) % N_DOM)[:, None]
    return jnp.where(filled, SLOTS, counts).astype(jnp.int32)


def with_ends(array, stream_key, smallest, top_value):
    longest = array.shape.index(max(array.shape))
    spots = []
    for shift in (0, 1):
        where = [jax.random.randint(jax.random.fold_in(stream_key, axis), (), 0, length) for axis, length in enumerate(array.shape)]
        where[longest] = (where[longest] + shift) % array.shape[longest]
        spots.append(tuple(where))
    return array.at[spots[0]].set(smallest).at[spots[1]].set(top_value)


def block_levels(own_key, dims, shards, smallest, largest):
    loudness, own = 1.0, jax.random.fold_in(own_key, 6)
    for axis_at, shards_of in shards:
        heights = jnp.exp(jax.random.uniform(jax.random.fold_in(own, axis_at), (shards_of,), jnp.float32, smallest / len(shards), largest / len(shards)))
        loudness = loudness * jnp.repeat(heights, dims[axis_at] // shards_of).reshape([-1 if axis == axis_at else 1 for axis in range(len(dims))])
    return loudness


def noise(key, extent, spread, reach, shards=(), kind=jnp.bfloat16):
    entries = spread * jax.random.normal(key, extent, jnp.float32)
    if shards:
        entries = entries * block_levels(key, extent, shards, -0.22, 0.18)
    return jnp.clip(entries, -reach, reach).astype(kind)


def setup_inputs(seed: int = 0) -> dict:
    streams_of = jax.random.split(jax.random.key(seed), 10)
    features = noise(streams_of[0], (VERTICES, F), 1.0, 6.0, ((0, 32),))
    weight = noise(streams_of[1], (F, F), F ** -0.5, 0.25)
    cotangent = noise(streams_of[2], (VERTICES, F), 1.0, 6.0, ((0, 32),))
    tile_values = noise(streams_of[3], (TILES, TILE, TILE), (TILES_DEV * TILE * TILE // R_DEV) ** -0.5, 0.21875, ((0, 32),))
    tile_rows = with_ends(jax.random.randint(streams_of[4], (TILES,), 0, ROW_BLOCKS), jax.random.fold_in(streams_of[4], 1), 0, ROW_BLOCKS - 1).astype(jnp.int32)
    tile_cols = draw_tile_cols(jax.random.fold_in(streams_of[9], 71), 0)
    hub_rows = with_ends(jax.random.randint(streams_of[6], (HUBS,), 0, R_DEV), jax.random.fold_in(streams_of[6], 1), 0, R_DEV - 1).astype(jnp.int32)
    send_rows = with_ends(jax.random.randint(streams_of[7], (N_DOM, N_DOM, SLOTS), 0, R_DEV), jax.random.fold_in(streams_of[7], 1), 0, R_DEV - 1).astype(jnp.int32)
    send_count = draw_send_count(jax.random.fold_in(streams_of[9], 71), 0)
    return {"features": features, "weight": weight, "cotangent": cotangent, "tile_values": tile_values, "tile_rows": tile_rows, "tile_cols": tile_cols, "hub_rows": hub_rows, "send_rows": send_rows, "send_count": send_count}


def reference(features, weight, cotangent, tile_values, tile_rows, tile_cols, hub_rows, send_rows, send_count):
    bases = jnp.arange(N_DOM, dtype=jnp.int32) * R_DEV
    hub_global = (hub_rows.reshape(N_DOM, HUBS_DEV) + bases[:, None]).reshape(-1)
    slot_ids = jnp.arange(SLOTS, dtype=jnp.int32)

    def aggregate(feat_full):
        hub_all = feat_full[hub_global]

        def one_device(device):
            own_rows = lax.dynamic_slice_in_dim(feat_full, (device * R_DEV).astype(jnp.int32), R_DEV, 0)
            sources = send_rows[:, device, :] + bases[:, None]
            live_slots = slot_ids[None, :] < send_count[:, device][:, None]
            incoming = jnp.where(live_slots.reshape(-1)[:, None], feat_full[sources.reshape(-1)], jnp.zeros((), feat_full.dtype))
            table = jnp.concatenate([own_rows, hub_all, incoming], axis=0).reshape(EXT_BLOCKS, TILE, F)
            start = (device * TILES_DEV).astype(jnp.int32)
            values = lax.dynamic_slice_in_dim(tile_values, start, TILES_DEV, 0).astype(jnp.float32)
            rows_here = lax.dynamic_slice_in_dim(tile_rows, start, TILES_DEV, 0)
            cols_here = lax.dynamic_slice_in_dim(tile_cols, start, TILES_DEV, 0)
            products = jnp.einsum('kij,kjf->kif', values, table[cols_here], precision=lax.Precision.HIGHEST)
            summed = jnp.zeros((ROW_BLOCKS, TILE, F), feat_full.dtype).at[rows_here].add(products)
            return summed.reshape(R_DEV, F)
        return lax.map(one_device, jnp.arange(N_DOM, dtype=jnp.int32)).reshape(-1, F)
    agg_full, pullback = jax.vjp(aggregate, features.astype(jnp.float32))
    aggregated = agg_full.astype(jnp.bfloat16)
    pre_act = jnp.dot(aggregated, weight, preferred_element_type=jnp.float32)
    sigmoid_pre = jax.nn.sigmoid(pre_act)
    output = (pre_act * sigmoid_pre).astype(jnp.bfloat16)
    grad_pre = (cotangent.astype(jnp.float32) * sigmoid_pre * (1.0 + pre_act * (1.0 - sigmoid_pre))).astype(jnp.bfloat16)
    grad_weight = jnp.dot(aggregated.T, grad_pre, preferred_element_type=jnp.float32) * float(VERTICES) ** (-0.5)
    grad_agg = jnp.dot(grad_pre, weight.T, preferred_element_type=jnp.float32).astype(jnp.bfloat16)
    grad_features = pullback(grad_agg.astype(jnp.float32))[0].astype(jnp.bfloat16)
    return (output, grad_features, grad_weight)
```

```python
import functools

import jax
import jax.numpy as jnp
from jax import lax
from jax.experimental import pallas as pl
from jax.experimental.pallas import tpu as pltpu
from jax.sharding import PartitionSpec as P

LOC_TILES = 64
LANES = 128
VMEM = pl.BlockSpec(memory_space=pltpu.VMEM)
SMEM = pl.BlockSpec(memory_space=pltpu.SMEM)


def rows_at(block, size):
    return pl.ds(pl.multiple_of(block * size, size), size)


def params(limit):
    return pltpu.CompilerParams(vmem_limit_bytes=limit)


def pack_kernel(n, slots, hubs, send_rows, send_count, hub_rows, feats, out, select):
    rows, width = feats.shape
    chunks = width // LANES
    sub = lax.broadcasted_iota(jnp.int32, (2 * slots, LANES), 0)
    lane = lax.broadcasted_iota(jnp.int32, (2 * slots, LANES), 1)

    def put(at, column):
        for part in range(rows // LANES):
            hit = jnp.where(column == lane + part * LANES, 1.0, 0.0)
            select[rows_at(at, 2 * slots), part * LANES : (part + 1) * LANES] = hit.astype(jnp.bfloat16)

    column = jnp.zeros((2 * slots, LANES), jnp.int32)
    for row in range(hubs * chunks):
        column = jnp.where(sub == row, hub_rows[row % hubs], column)
    put(0, column)

    def pair(q, _):
        column = jnp.full((2 * slots, LANES), -1, jnp.int32)
        for half in range(2):
            dest = 2 * q + half
            count = send_count[0, dest]
            for k in range(slots):
                row = jnp.where(k < count, send_rows[0, dest, k], -1)
                column = jnp.where(sub == half * slots + k, row, column)
        put(q + 1, column)
        return 0

    lax.fori_loop(0, n // 2, pair, 0)
    group = sub // hubs
    found = jnp.dot(select[0 : 2 * slots, :], feats[...], preferred_element_type=jnp.float32)
    hub = jnp.zeros((hubs * chunks, LANES), jnp.float32)
    for c in range(chunks):
        hub = jnp.where(group == c, found[:, c * LANES : (c + 1) * LANES], hub)
    hub = hub.astype(jnp.bfloat16)
    per = 128 // slots

    def many(b, _):
        got = jnp.dot(
            select[pl.ds(pl.multiple_of(b * 128 + 2 * slots, 16), 128), :],
            feats[...],
            preferred_element_type=jnp.float32,
        )
        for s in range(per):
            dest = b * per + s
            out[dest, 0:16, :] = hub
            mine = got[s * slots : (s + 1) * slots, :]
            for c in range(0, chunks, 2):
                both = jnp.concatenate(
                    [mine[:, c * LANES : (c + 1) * LANES], mine[:, (c + 1) * LANES : (c + 2) * LANES]], axis=0
                )
                out[dest, 16 + c * slots : 16 + (c + 2) * slots, :] = both.astype(jnp.bfloat16)
        return 0

    lax.fori_loop(0, n // per, many, 0)


def pack_rows(n, send_rows, send_count, hub_rows, features):
    slots, hubs = send_rows.shape[2], hub_rows.shape[0]
    rows, width = features.shape
    packed = (slots + hubs) * width // LANES
    return pl.pallas_call(
        functools.partial(pack_kernel, n, slots, hubs),
        out_shape=jax.ShapeDtypeStruct((n, packed, LANES), jnp.bfloat16),
        in_specs=[SMEM, SMEM, SMEM, VMEM],
        out_specs=VMEM,
        scratch_shapes=[pltpu.VMEM((n * slots + 2 * slots, rows), jnp.bfloat16)],
        compiler_params=params(16 << 20),
        name="pack_rows",
    )(send_rows, send_count, hub_rows, features)


def near_forward_kernel(count, tile_rows, tile_cols, tiles, feats, total):
    size = tiles.shape[1]
    blocks = feats.shape[0] // size
    total[...] = jnp.zeros_like(total)

    def one(t, _):
        row, col = tile_rows[t], tile_cols[t]

        @pl.when(col < blocks)
        def _():
            total[rows_at(row, size), :] += jnp.dot(
                tiles[t], feats[rows_at(col, size), :], preferred_element_type=jnp.float32
            )

        return 0

    lax.fori_loop(0, count, one, 0)


def near_forward(tile_rows, tile_cols, tiles, features):
    return pl.pallas_call(
        functools.partial(near_forward_kernel, LOC_TILES),
        out_shape=jax.ShapeDtypeStruct(features.shape, jnp.float32),
        in_specs=[SMEM, SMEM, VMEM, VMEM],
        out_specs=VMEM,
        compiler_params=params(16 << 20),
        cost_estimate=pl.CostEstimate(flops=4 << 30, bytes_accessed=8 << 20, transcendentals=0),
        name="near_forward",
    )(tile_rows, tile_cols, tiles, features)


def unpack_slots(n, slots, chunks, packed, into, at):
    def pair(q, _):
        for c in range(0, chunks, 2):
            spot = slice(16 + c * slots, 16 + (c + 2) * slots)
            first = packed[2 * q, spot, :].astype(jnp.float32)
            second = packed[2 * q + 1, spot, :].astype(jnp.float32)
            for half in range(2):
                part = slice(half * slots, (half + 1) * slots)
                both = jnp.concatenate([first[part], second[part]], axis=0).astype(jnp.bfloat16)
                where = pl.ds(pl.multiple_of(at + q * 2 * slots, 2 * slots), 2 * slots)
                into[where, (c + half) * LANES : (c + half + 1) * LANES] = both
        return 0

    lax.fori_loop(0, n // 2, pair, 0)


def forward_kernel(
    n, slots, hubs, tile_rows, tile_cols, parity, tiles, received, near, weight, cotangent,
    output, grad_agg, keep, give, table, total, agg, grad_pre,
):
    size = tiles.shape[1]
    rows, width = near.shape
    chunks = width // LANES
    blocks = rows // size

    def four(q, _):
        parts = [received[4 * q + u, 0:16, :].astype(jnp.float32) for u in range(4)]
        for c in range(chunks):
            quad = jnp.concatenate([part[c * hubs : (c + 1) * hubs] for part in parts], axis=0)
            table[rows_at(q, 16), c * LANES : (c + 1) * LANES] = quad.astype(jnp.bfloat16)
        return 0

    lax.fori_loop(0, n // 4, four, 0)
    unpack_slots(n, slots, chunks, received, table, n * hubs)
    total[...] = near[...]

    def add(t):
        row, col = tile_rows[t], tile_cols[t]
        total[rows_at(row, size), :] += jnp.dot(
            tiles[t], table[rows_at(col - blocks, size), :], preferred_element_type=jnp.float32
        )

    def hub_tile(t, _):
        @pl.when(tile_cols[t] >= blocks)
        def _():
            add(t)

        return 0

    def far_tile(t, _):
        add(t)
        return 0

    lax.fori_loop(0, LOC_TILES, hub_tile, 0)
    lax.fori_loop(LOC_TILES, tiles.shape[0], far_tile, 0)
    step = 256

    def dense(b, _):
        at = rows_at(b, step)
        here = total[at, :].astype(jnp.bfloat16)
        agg[at, :] = here
        pre = jnp.dot(here, weight[...], preferred_element_type=jnp.float32)
        sig = jax.nn.sigmoid(pre)
        output[at, :] = (pre * sig).astype(jnp.bfloat16)
        gp = (cotangent[at, :].astype(jnp.float32) * sig * (1.0 + pre * (1.0 - sig))).astype(jnp.bfloat16)
        grad_pre[at, :] = gp
        grad_agg[at, :] = lax.dot_general(
            gp, weight[...], (((1,), (1,)), ((), ())), preferred_element_type=jnp.float32
        ).astype(jnp.bfloat16)
        return 0

    lax.fori_loop(0, rows // step, dense, 0)
    half = width // 2
    scale = float(rows * n) ** -0.5
    mine = parity[0]
    for h, target in ((mine, keep), (1 - mine, give)):
        term = lax.dot_general(
            agg[:, pl.ds(pl.multiple_of(h * half, half), half)],
            grad_pre[...],
            (((0,), (0,)), ((), ())),
            preferred_element_type=jnp.float32,
        )
        target[...] = (term * scale).astype(target.dtype)


def forward(n, slots, hubs, tile_rows, tile_cols, parity, tiles, received, near, weight, cotangent):
    rows, width = near.shape
    table_rows = n * (slots + hubs)
    shape = jax.ShapeDtypeStruct
    return pl.pallas_call(
        functools.partial(forward_kernel, n, slots, hubs),
        out_shape=(
            shape((rows, width), jnp.bfloat16),
            shape((rows, width), jnp.bfloat16),
            shape((width // 2, width), jnp.float32),
            shape((width // 2, width), jnp.bfloat16),
        ),
        in_specs=[SMEM, SMEM, SMEM] + [VMEM] * 5,
        out_specs=(VMEM,) * 4,
        scratch_shapes=[
            pltpu.VMEM((table_rows, width), jnp.bfloat16),
            pltpu.VMEM((rows, width), jnp.float32),
            pltpu.VMEM((rows, width), jnp.bfloat16),
            pltpu.VMEM((rows, width), jnp.bfloat16),
        ],
        compiler_params=params(32 << 20),
        name="forward",
    )(tile_rows, tile_cols, parity, tiles, received, near, weight, cotangent)


def transposed_product(tile, block):
    return lax.dot_general(tile, block, (((0,), (0,)), ((), ())), preferred_element_type=jnp.float32)


def far_backward_kernel(n, slots, hubs, tile_rows, tile_cols, tiles, grad_agg, out, total):
    size = tiles.shape[1]
    rows, width = grad_agg.shape
    chunks = width // LANES
    blocks = rows // size
    total[...] = jnp.zeros_like(total)

    def add(t):
        row, col = tile_rows[t], tile_cols[t]
        total[rows_at(col - blocks, size), :] += transposed_product(tiles[t], grad_agg[rows_at(row, size), :])

    def hub_tile(t, _):
        @pl.when(tile_cols[t] >= blocks)
        def _():
            add(t)

        return 0

    def far_tile(t, _):
        add(t)
        return 0

    lax.fori_loop(0, LOC_TILES, hub_tile, 0)
    lax.fori_loop(LOC_TILES, tiles.shape[0], far_tile, 0)

    def two(q, _):
        both = total[pl.ds(pl.multiple_of(q * 2 * hubs, 2 * hubs), 2 * hubs), :]
        for u in range(2):
            mine = both[u * hubs : (u + 1) * hubs]
            out[2 * q + u, 0:16, :] = jnp.concatenate(
                [mine[:, c * LANES : (c + 1) * LANES] for c in range(chunks)], axis=0
            ).astype(jnp.bfloat16)
            halo = total[pl.ds(pl.multiple_of(n * hubs + (2 * q + u) * slots, slots), slots), :]
            for c in range(0, chunks, 2):
                pair = jnp.concatenate(
                    [halo[:, c * LANES : (c + 1) * LANES], halo[:, (c + 1) * LANES : (c + 2) * LANES]], axis=0
                )
                out[2 * q + u, 16 + c * slots : 16 + (c + 2) * slots, :] = pair.astype(jnp.bfloat16)
        return 0

    lax.fori_loop(0, n // 2, two, 0)


def far_backward(n, slots, hubs, tile_rows, tile_cols, tiles, grad_agg):
    width = grad_agg.shape[1]
    packed = (slots + hubs) * width // LANES
    return pl.pallas_call(
        functools.partial(far_backward_kernel, n, slots, hubs),
        out_shape=jax.ShapeDtypeStruct((n, packed, LANES), jnp.bfloat16),
        in_specs=[SMEM, SMEM, VMEM, VMEM],
        out_specs=VMEM,
        scratch_shapes=[pltpu.VMEM((n * (slots + hubs), width), jnp.float32)],
        compiler_params=params(16 << 20),
        name="far_backward",
    )(tile_rows, tile_cols, tiles, grad_agg)


def near_backward_kernel(n, slots, hubs, tile_rows, tile_cols, send_rows, send_count, hub_rows, tiles, grad_agg, total, spread):
    size = tiles.shape[1]
    rows, width = grad_agg.shape
    chunks = width // LANES
    blocks = rows // size
    total[...] = jnp.zeros_like(total)

    def one(t, _):
        row, col = tile_rows[t], tile_cols[t]

        @pl.when(col < blocks)
        def _():
            total[rows_at(col, size), :] += transposed_product(tiles[t], grad_agg[rows_at(row, size), :])

        return 0

    lax.fori_loop(0, LOC_TILES, one, 0)
    lane = lax.broadcasted_iota(jnp.int32, (16, LANES), 1)
    sub = lax.broadcasted_iota(jnp.int32, (16, LANES), 0)

    def put(part, targets):
        def rows_of(b, _):
            hit = jnp.where(targets == sub + b * 16, 1.0, 0.0)
            spread[rows_at(b, 16), part * LANES : (part + 1) * LANES] = hit.astype(jnp.bfloat16)
            return 0

        lax.fori_loop(0, rows // 16, rows_of, 0, unroll=4)

    per = LANES // slots
    for part in range(n * slots // LANES):

        def dest(s, targets, part=part):
            count = send_count[0, part * per + s]
            for k in range(slots):
                row = jnp.where(k < count, send_rows[0, part * per + s, k], -1)
                targets = jnp.where(lane == s * slots + k, row, targets)
            return targets

        put(part, lax.fori_loop(0, per, dest, jnp.full((16, LANES), -1, jnp.int32)))
    targets = jnp.full((16, LANES), -1, jnp.int32)
    for at in range(2 * hubs * chunks):
        targets = jnp.where(lane == at, hub_rows[at % hubs], targets)
    put(n * slots // LANES, targets)


def near_backward(n, slots, hubs, tile_rows, tile_cols, send_rows, send_count, hub_rows, tiles, grad_agg):
    rows, width = grad_agg.shape
    return pl.pallas_call(
        functools.partial(near_backward_kernel, n, slots, hubs),
        out_shape=(
            jax.ShapeDtypeStruct((rows, width), jnp.float32),
            jax.ShapeDtypeStruct((rows, n * slots + LANES), jnp.bfloat16),
        ),
        in_specs=[SMEM] * 5 + [VMEM] * 2,
        out_specs=(VMEM, VMEM),
        compiler_params=params(16 << 20),
        cost_estimate=pl.CostEstimate(flops=4 << 30, bytes_accessed=8 << 20, transcendentals=0),
        name="near_backward",
    )(tile_rows, tile_cols, send_rows, send_count, hub_rows, tiles, grad_agg)


def collect_kernel(n, slots, hubs, near, spread, returned, out, table):
    rows, width = near.shape
    chunks = width // LANES
    unpack_slots(n, slots, chunks, returned, table, 0)
    hub = lax.fori_loop(
        0,
        n,
        lambda s, held: held + returned[s, 0:16, :].astype(jnp.float32),
        jnp.zeros((16, LANES), jnp.float32),
        unroll=4,
    )
    group = lax.broadcasted_iota(jnp.int32, (16, LANES), 0) // hubs
    base = n * slots
    table[base : base + LANES, :] = jnp.zeros((LANES, width), jnp.bfloat16)
    upper = hub.astype(jnp.bfloat16).astype(jnp.float32)
    for at, part in ((0, upper), (16, hub - upper)):
        for c in range(chunks):
            table[base + at : base + at + 16, c * LANES : (c + 1) * LANES] = jnp.where(
                group == c, part, 0.0
            ).astype(jnp.bfloat16)

    def block(b, _):
        at = rows_at(b, 256)
        more = jnp.dot(spread[at, :], table[...], preferred_element_type=jnp.float32)
        out[at, :] = (near[at, :] + more).astype(jnp.bfloat16)
        return 0

    lax.fori_loop(0, rows // 256, block, 0)


def collect(n, slots, hubs, near, spread, returned):
    rows, width = near.shape
    return pl.pallas_call(
        functools.partial(collect_kernel, n, slots, hubs),
        out_shape=jax.ShapeDtypeStruct((rows, width), jnp.bfloat16),
        in_specs=[VMEM] * 3,
        out_specs=VMEM,
        scratch_shapes=[pltpu.VMEM((n * slots + LANES, width), jnp.bfloat16)],
        compiler_params=params(16 << 20),
        name="collect",
    )(near, spread, returned)


def swap_cores(x, n):
    return lax.ppermute(x, "dom", [(i, i ^ 1) for i in range(n)])


def exchange(x, groups=None):
    return lax.all_to_all(x, "dom", split_axis=0, concat_axis=0, tiled=True, axis_index_groups=groups)


def per_device(
    features, weight, cotangent, tile_values, tile_rows, tile_cols, hub_rows, send_rows, send_count
):
    n = lax.axis_size("dom")
    slots, hubs = send_rows.shape[2], hub_rows.shape[0]
    width = features.shape[1]
    parity = lax.rem(lax.axis_index("dom"), 2)
    same_core = [[2 * chip + core for chip in range(n // 2)] for core in range(2)]

    packed = pack_rows(n, send_rows, send_count, hub_rows, features)
    received = exchange(packed)
    near = near_forward(tile_rows, tile_cols, tile_values, features)
    output, grad_agg, keep, give = forward(
        n, slots, hubs, tile_rows, tile_cols, parity.reshape(1), tile_values, received, near, weight, cotangent
    )
    half = keep + swap_cores(give, n).astype(jnp.float32)
    share = half.shape[0] // (n // 2)
    terms = exchange(half.astype(jnp.bfloat16).reshape(n // 2, share, width), same_core)

    far = far_backward(n, slots, hubs, tile_rows, tile_cols, tile_values, grad_agg)
    returned = exchange(far)
    near_grad, spread = near_backward(
        n, slots, hubs, tile_rows, tile_cols, send_rows, send_count, hub_rows, tile_values, grad_agg
    )
    summed = jnp.sum(terms.astype(jnp.float32), axis=0).astype(jnp.bfloat16)
    mine = exchange(jnp.broadcast_to(summed, terms.shape), same_core).reshape(half.shape)
    other = swap_cores(mine, n)
    grad_features = collect(n, slots, hubs, near_grad, spread, returned)
    first = jnp.where(parity == 0, mine, other)
    second = jnp.where(parity == 0, other, mine)
    grad_weight = jnp.concatenate([first, second], axis=0).astype(jnp.float32)
    return (output, grad_features, grad_weight)


def solution(mesh):
    placed = (
        P("dom", None),
        P(),
        P("dom", None),
        P("dom", None, None),
        P("dom"),
        P("dom"),
        P("dom"),
        P("dom", None, None),
        P("dom", None),
    )
    return jax.shard_map(
        per_device,
        mesh=mesh,
        in_specs=placed,
        out_specs=(P("dom", None), P("dom", None), P()),
        check_vma=False,
    )
```

```python
import functools

import jax
import jax.numpy as jnp
from jax import lax
from jax.experimental import pallas as pl
from jax.experimental.pallas import tpu as pltpu
from jax.sharding import PartitionSpec as P

LOC_TILES = 64
LANES = 128
SUBS = 16
NONE = 255
KEYS = 32
LIST = 64
UNROLL = 4
NEAR_FWD, FAR_FWD, NEAR_BWD, FAR_BWD = range(4)
COUNTS = 4 * LIST
PLAN = COUNTS + LANES
VMEM = pl.BlockSpec(memory_space=pltpu.VMEM)
HBM = pl.BlockSpec(memory_space=pltpu.HBM)
DMA = pltpu.SemaphoreType.DMA
BF16, F32, I32 = jnp.bfloat16, jnp.float32, jnp.int32


def rows_at(block, size):
    return pl.ds(pl.multiple_of(block * size, size), size)


def params(limit):
    return pltpu.CompilerParams(vmem_limit_bytes=limit)


def in_hbm(*arrays):
    return [pltpu.with_memory_space_constraint(a, pltpu.HBM) for a in arrays]


def cost(flops, moved):
    return pl.CostEstimate(flops=flops, bytes_accessed=moved, transcendentals=0)


def start(source, target, sem):
    copy = pltpu.make_async_copy(source, target, sem)
    copy.start()
    return copy


def pack_kernel(
    n, slots, hubs, send_rows_in, send_count_in, hub_rows_in, feats_in, out,
    send_rows, send_count, hub_rows, feats, select, staged, sems, out_sems,
):
    rows, width = feats.shape
    chunks = width // LANES
    copies = [
        start(a, b, sems.at[i])
        for i, (a, b) in enumerate(
            (
                (send_rows_in, send_rows),
                (send_count_in, send_count),
                (hub_rows_in, hub_rows),
                (feats_in, feats),
            )
        )
    ]
    sub = lax.broadcasted_iota(I32, (2 * slots, LANES), 0)
    lane = lax.broadcasted_iota(I32, (2 * slots, LANES), 1)
    for copy in copies[:3]:
        copy.wait()

    def put(at, column):
        for part in range(rows // LANES):
            hit = jnp.where(column == lane + part * LANES, 1.0, 0.0)
            select[rows_at(at, 2 * slots), part * LANES : (part + 1) * LANES] = hit.astype(BF16)

    column = jnp.zeros((2 * slots, LANES), I32)
    for row in range(hubs * chunks):
        column = jnp.where(sub == row, hub_rows[row % hubs], column)
    put(0, column)

    def pair(q, _):
        column = jnp.full((2 * slots, LANES), -1, I32)
        for half in range(2):
            dest = 2 * q + half
            count = send_count[0, dest]
            for k in range(slots):
                row = jnp.where(k < count, send_rows[0, k, dest], -1)
                column = jnp.where(sub == half * slots + k, row, column)
        put(q + 1, column)
        return 0

    lax.fori_loop(0, n // 2, pair, 0, unroll=2)
    copies[3].wait()
    group = sub // hubs
    found = jnp.dot(select[0 : 2 * slots, :], feats[...], preferred_element_type=F32)
    hub = jnp.zeros((hubs * chunks, LANES), F32)
    for c in range(chunks):
        hub = jnp.where(group == c, found[:, c * LANES : (c + 1) * LANES], hub)
    hub = hub.astype(BF16)
    per = LANES // slots
    sent = []
    for b in range(n // per):
        got = jnp.dot(
            select[b * LANES + 2 * slots : (b + 1) * LANES + 2 * slots, :], feats[...], preferred_element_type=F32
        )
        for s in range(per):
            dest = b * per + s
            staged[dest, 0:SUBS, :] = hub
            mine = got[s * slots : (s + 1) * slots, :]
            for c in range(0, chunks, 2):
                both = jnp.concatenate(
                    [mine[:, c * LANES : (c + 1) * LANES], mine[:, (c + 1) * LANES : (c + 2) * LANES]], axis=0
                )
                staged[dest, SUBS + c * slots : SUBS + (c + 2) * slots, :] = both.astype(BF16)
        group_of = pl.ds(b * per, per)
        sent.append(start(staged.at[group_of], out.at[group_of], out_sems.at[b]))
    for copy in sent:
        copy.wait()


def pack_rows(n, send_rows, send_count, hub_rows, features):
    slots, hubs = send_rows.shape[1], hub_rows.shape[0]
    rows, width = features.shape
    packed = (n, (slots + hubs) * width // LANES, LANES)
    return pl.pallas_call(
        functools.partial(pack_kernel, n, slots, hubs),
        out_shape=pltpu.HBM(packed, BF16),
        in_specs=[HBM] * 4,
        out_specs=HBM,
        scratch_shapes=[
            pltpu.SMEM(send_rows.shape, I32),
            pltpu.SMEM(send_count.shape, I32),
            pltpu.SMEM(hub_rows.shape, I32),
            pltpu.VMEM((rows, width), BF16),
            pltpu.VMEM((n * slots + 2 * slots, rows), BF16),
            pltpu.VMEM(packed, BF16),
            DMA((4,)),
            DMA((n * slots // LANES,)),
        ],
        compiler_params=params(16 << 20),
        name="pack_rows",
    )(*in_hbm(send_rows, send_count, hub_rows, features))


def make_plan(tile_rows, tile_cols, blocks, plan, waiting):
    def clear(i, _):
        waiting[i] = NONE
        return 0

    lax.fori_loop(0, 4 * KEYS, clear, 0, unroll=8)
    for kind in range(4):
        plan[COUNTS + kind] = 0

    def add(kind, key, t):
        slot = kind * KEYS + key
        first, count = waiting[slot], plan[COUNTS + kind]
        pair = first != NONE
        plan[kind * LIST + count] = (key << 16) | (first << 8) | t
        plan[COUNTS + kind] = count + pair.astype(I32)
        waiting[slot] = jnp.where(pair, NONE, t)

    def tile(t, _):
        row, col = tile_rows[t], tile_cols[t]
        far = (col >= blocks).astype(I32)
        add(NEAR_FWD + far, row, t)
        add(NEAR_BWD + far, col - blocks * far, t)
        return 0

    lax.fori_loop(0, tile_rows.shape[0], tile, 0)
    for kind in range(4):

        def left(key, count, kind=kind):
            first = waiting[kind * KEYS + key]
            plan[kind * LIST + count] = (key << 16) | (first << 8) | NONE
            return count + (first != NONE).astype(I32)

        count = lax.fori_loop(0, KEYS, left, plan[COUNTS + kind])
        plan[COUNTS + kind] = count
        for u in range(UNROLL):
            plan[kind * LIST + count + u] = (NONE << 8) | NONE


def run_plan(kind, plan, tiles, source_of, source, total, transposed):
    size, last = tiles.shape[1], tiles.shape[0] - 1
    axis = 0 if transposed else 1

    def group(g, _):
        for u in range(UNROLL):
            word = plan[kind * LIST + g * UNROLL + u]
            key, picks = word >> 16, ((word >> 8) & 255, word & 255)
            left, right = [], []
            for pick in picks:
                t = jnp.minimum(pick, last)
                left.append(jnp.where(pick == NONE, jnp.zeros((size, size), BF16), tiles[t]))
                right.append(source[rows_at(source_of(t), size), :])
            total[rows_at(key, size), :] += lax.dot_general(
                jnp.concatenate(left, axis=axis),
                jnp.concatenate(right, axis=0),
                (((axis,), (0,)), ((), ())),
                preferred_element_type=F32,
            )
        return 0

    lax.fori_loop(0, (plan[COUNTS + kind] + UNROLL - 1) // UNROLL, group, 0)


def near_forward_kernel(
    tile_rows_in, tile_cols_in, tiles, feats_in, near_out, plan_out,
    tile_rows, tile_cols, feats, total, plan, waiting, sems,
):
    rows, width = feats.shape
    blocks = rows // tiles.shape[1]
    copies = [
        start(a, b, sems.at[i])
        for i, (a, b) in enumerate(((tile_rows_in, tile_rows), (tile_cols_in, tile_cols), (feats_in, feats)))
    ]
    total[...] = jnp.zeros_like(total)
    copies[0].wait()
    copies[1].wait()
    make_plan(tile_rows, tile_cols, blocks, plan, waiting)
    sent = start(plan, plan_out, sems.at[0])
    copies[2].wait()
    run_plan(NEAR_FWD, plan, tiles, lambda t: jnp.minimum(tile_cols[t], blocks - 1), feats, total, False)
    last = start(total, near_out, sems.at[1])
    sent.wait()
    last.wait()


def near_forward(tile_rows, tile_cols, tiles, features):
    rows, width = features.shape
    return pl.pallas_call(
        near_forward_kernel,
        out_shape=(pltpu.HBM((rows, width), F32), pltpu.HBM((PLAN,), I32)),
        in_specs=[HBM, HBM, VMEM, HBM],
        out_specs=(HBM, HBM),
        scratch_shapes=[
            pltpu.SMEM(tile_rows.shape, I32),
            pltpu.SMEM(tile_cols.shape, I32),
            pltpu.VMEM((rows, width), BF16),
            pltpu.VMEM((rows, width), F32),
            pltpu.SMEM((PLAN,), I32),
            pltpu.SMEM((4 * KEYS,), I32),
            DMA((3,)),
        ],
        compiler_params=params(12 << 20),
        cost_estimate=cost(4 << 30, 8 << 20),
        name="near_forward",
    )(*in_hbm(tile_rows, tile_cols), tiles, *in_hbm(features))


def unpack_slots(n, slots, chunks, packed, into, at):
    def pair(q, _):
        for c in range(0, chunks, 2):
            spot = slice(SUBS + c * slots, SUBS + (c + 2) * slots)
            first = packed[2 * q, spot, :].astype(F32)
            second = packed[2 * q + 1, spot, :].astype(F32)
            for half in range(2):
                part = slice(half * slots, (half + 1) * slots)
                both = jnp.concatenate([first[part], second[part]], axis=0).astype(BF16)
                where = pl.ds(pl.multiple_of(at + q * 2 * slots, 2 * slots), 2 * slots)
                into[where, (c + half) * LANES : (c + half + 1) * LANES] = both
        return 0

    lax.fori_loop(0, n // 2, pair, 0, unroll=4)


def reversed_bits(value, bits):
    out = jnp.zeros((), I32)
    for bit in range(bits):
        out = out | (((value >> bit) & 1) << (bits - 1 - bit))
    return out


def halvings(n, width):
    steps = 0
    while 2 << steps <= n and width >> (steps + 1) >= SUBS:
        steps += 1
    return steps


def forward_kernel(
    n, slots, hubs, tile_rows_in, tile_cols_in, plan_in, tiles, received, near_in, weight_in, cot_in,
    output, grad_pre_out, keep, give,
    tile_rows, tile_cols, plan, table, total, near, weight, cot, agg, grad_pre, out, sems, near_sems, cot_sems, out_sems, gp_sems,
):
    size = tiles.shape[1]
    rows, width = near.shape
    chunks = width // LANES
    blocks = rows // size
    step = 256
    steps = rows // step
    index = [
        start(a, b, sems.at[i])
        for i, (a, b) in enumerate(((plan_in, plan), (tile_rows_in, tile_rows), (tile_cols_in, tile_cols)))
    ]
    weight_copy = start(weight_in, weight, sems.at[3])
    pieces = [pl.ds(b * step, step) for b in range(steps)]
    near_copies = [start(near_in.at[at], near.at[at], near_sems.at[b]) for b, at in enumerate(pieces)]
    cot_copies = [start(cot_in.at[at], cot.at[at], cot_sems.at[b]) for b, at in enumerate(pieces)]
    total[...] = jnp.zeros_like(total)

    def four(q, _):
        parts = [received[4 * q + u, 0:SUBS, :].astype(F32) for u in range(4)]
        for c in range(chunks):
            quad = jnp.concatenate([part[c * hubs : (c + 1) * hubs] for part in parts], axis=0)
            table[rows_at(q, SUBS), c * LANES : (c + 1) * LANES] = quad.astype(BF16)
        return 0

    lax.fori_loop(0, n // 4, four, 0, unroll=2)
    unpack_slots(n, slots, chunks, received, table, n * hubs)
    for copy in index:
        copy.wait()
    run_plan(FAR_FWD, plan, tiles, lambda t: jnp.maximum(tile_cols[t] - blocks, 0), table, total, False)
    weight_copy.wait()
    sent = []
    for b, at in enumerate(pieces):
        near_copies[b].wait()
        cot_copies[b].wait()
        here = (total[at, :] + near[at, :]).astype(BF16)
        agg[at, :] = here
        pre = jnp.dot(here, weight[...], preferred_element_type=F32)
        sig = jax.nn.sigmoid(pre)
        out[at, :] = (pre * sig).astype(BF16)
        grad_pre[at, :] = (cot[at, :].astype(F32) * sig * (1.0 + pre * (1.0 - sig))).astype(BF16)
        sent.append(start(out.at[at], output.at[at], out_sems.at[b]))
        sent.append(start(grad_pre.at[at], grad_pre_out.at[at], gp_sems.at[b]))
    scale = float(rows * n) ** -0.5
    term = total.at[pl.ds(0, width)]
    for c in range(0, width, 256):
        term[c : c + 256, :] = (
            lax.dot_general(
                agg[:, c : c + 256], grad_pre[...], (((0,), (0,)), ((), ())), preferred_element_type=F32
            )
            * scale
        )
    bits = halvings(n, width)
    unit = width >> bits
    mine = reversed_bits(lax.axis_index("dom"), bits)
    half = 1 << (bits - 1)
    for b in range(half):
        spot = slice(b * unit, (b + 1) * unit)
        keep[spot, :] = term[rows_at(mine ^ b, unit), :]
        give[spot, :] = term[rows_at(mine ^ (b + half), unit), :].astype(BF16)
    for copy in sent:
        copy.wait()


def forward(n, slots, hubs, tile_rows, tile_cols, plan, tiles, received, near, weight, cotangent):
    rows, width = near.shape
    steps = rows // 256
    shape = jax.ShapeDtypeStruct
    return pl.pallas_call(
        functools.partial(forward_kernel, n, slots, hubs),
        out_shape=(
            pltpu.HBM((rows, width), BF16),
            pltpu.HBM((rows, width), BF16),
            shape((width // 2, width), F32),
            shape((width // 2, width), BF16),
        ),
        in_specs=[HBM, HBM, HBM, VMEM, VMEM, HBM, HBM, HBM],
        out_specs=(HBM, HBM, VMEM, VMEM),
        scratch_shapes=[
            pltpu.SMEM(tile_rows.shape, I32),
            pltpu.SMEM(tile_cols.shape, I32),
            pltpu.SMEM((PLAN,), I32),
            pltpu.VMEM((n * (slots + hubs), width), BF16),
            pltpu.VMEM((rows, width), F32),
            pltpu.VMEM((rows, width), F32),
            pltpu.VMEM((width, width), BF16),
            pltpu.VMEM((rows, width), BF16),
            pltpu.VMEM((rows, width), BF16),
            pltpu.VMEM((rows, width), BF16),
            pltpu.VMEM((rows, width), BF16),
            DMA((4,)),
            DMA((steps,)),
            DMA((steps,)),
            DMA((steps,)),
            DMA((steps,)),
        ],
        compiler_params=params(28 << 20),
        cost_estimate=cost(8 << 30, 16 << 20),
        name="forward",
    )(*in_hbm(tile_rows, tile_cols, plan), tiles, received, *in_hbm(near, weight, cotangent))


def far_backward_kernel(
    n, slots, hubs, tile_rows_in, plan_in, tiles, grad_pre_in, weight_in, out, grad_agg_out,
    tile_rows, plan, grad_pre, weight, grad_agg, total, staged, sems, in_sems, out_sems,
):
    rows, width = grad_pre.shape
    chunks = width // LANES
    step = 512
    pieces = [pl.ds(at, step) for at in range(0, rows, step)]
    weight_copy = start(weight_in, weight, sems.at[0])
    copies = [start(grad_pre_in.at[at], grad_pre.at[at], in_sems.at[b]) for b, at in enumerate(pieces)]
    index = [start(plan_in, plan, sems.at[1]), start(tile_rows_in, tile_rows, sems.at[2])]
    total[...] = jnp.zeros_like(total)
    weight_copy.wait()
    sent = []
    for b, at in enumerate(pieces):
        copies[b].wait()
        grad_agg[at, :] = lax.dot_general(
            grad_pre[at, :], weight[...], (((1,), (1,)), ((), ())), preferred_element_type=F32
        ).astype(BF16)
        sent.append(start(grad_agg.at[at], grad_agg_out.at[at], out_sems.at[b]))
    for copy in index:
        copy.wait()
    run_plan(FAR_BWD, plan, tiles, lambda t: tile_rows[t], grad_agg, total, True)

    def two(q, _):
        both = total[rows_at(q, 2 * hubs), :]
        for u in range(2):
            mine = both[u * hubs : (u + 1) * hubs]
            staged[2 * q + u, 0:SUBS, :] = jnp.concatenate(
                [mine[:, c * LANES : (c + 1) * LANES] for c in range(chunks)], axis=0
            ).astype(BF16)
            halo = total[pl.ds(pl.multiple_of(n * hubs + (2 * q + u) * slots, slots), slots), :]
            for c in range(0, chunks, 2):
                pair = jnp.concatenate(
                    [halo[:, c * LANES : (c + 1) * LANES], halo[:, (c + 1) * LANES : (c + 2) * LANES]], axis=0
                )
                staged[2 * q + u, SUBS + c * slots : SUBS + (c + 2) * slots, :] = pair.astype(BF16)
        return 0

    lax.fori_loop(0, n // 2, two, 0, unroll=2)
    sent.append(start(staged, out, sems.at[0]))
    for copy in sent:
        copy.wait()


def far_backward(n, slots, hubs, tile_rows, plan, tiles, grad_pre, weight):
    rows, width = grad_pre.shape
    packed = (n, (slots + hubs) * width // LANES, LANES)
    return pl.pallas_call(
        functools.partial(far_backward_kernel, n, slots, hubs),
        out_shape=(pltpu.HBM(packed, BF16), pltpu.HBM((rows, width), BF16)),
        in_specs=[HBM, HBM, VMEM, HBM, HBM],
        out_specs=(HBM, HBM),
        scratch_shapes=[
            pltpu.SMEM(tile_rows.shape, I32),
            pltpu.SMEM((PLAN,), I32),
            pltpu.VMEM((rows, width), BF16),
            pltpu.VMEM((width, width), BF16),
            pltpu.VMEM((rows, width), BF16),
            pltpu.VMEM((n * (slots + hubs), width), F32),
            pltpu.VMEM(packed, BF16),
            DMA((3,)),
            DMA((rows // 512,)),
            DMA((rows // 512,)),
        ],
        compiler_params=params(16 << 20),
        cost_estimate=cost(4 << 30, 8 << 20),
        name="far_backward",
    )(*in_hbm(tile_rows, plan), tiles, *in_hbm(grad_pre, weight))


def near_backward_kernel(
    n, slots, hubs, tile_rows_in, plan_in, send_rows_in, send_count_in, hub_rows_in, tiles, grad_agg_in, total_out, spread_out,
    tile_rows, plan, send_rows, send_count, hub_rows, grad_agg, total, spread, sems,
):
    rows, width = grad_agg.shape
    chunks = width // LANES
    copies = [
        start(a, b, sems.at[i])
        for i, (a, b) in enumerate(
            (
                (tile_rows_in, tile_rows),
                (plan_in, plan),
                (send_rows_in, send_rows),
                (send_count_in, send_count),
                (hub_rows_in, hub_rows),
                (grad_agg_in, grad_agg),
            )
        )
    ]
    total[...] = jnp.zeros_like(total)
    for copy in copies:
        copy.wait()
    run_plan(NEAR_BWD, plan, tiles, lambda t: tile_rows[t], grad_agg, total, True)
    sent = start(total, total_out, sems.at[0])
    lane = lax.broadcasted_iota(I32, (SUBS, LANES), 1)
    sub = lax.broadcasted_iota(I32, (SUBS, LANES), 0)

    def put(part, targets):
        def rows_of(b, _):
            hit = jnp.where(targets == sub + b * SUBS, 1.0, 0.0)
            spread[rows_at(b, SUBS), part * LANES : (part + 1) * LANES] = hit.astype(BF16)
            return 0

        lax.fori_loop(0, rows // SUBS, rows_of, 0, unroll=8)

    per = LANES // slots
    for part in range(n * slots // LANES):

        def dest(s, targets, part=part):
            count = send_count[0, part * per + s]
            for k in range(slots):
                row = jnp.where(k < count, send_rows[0, k, part * per + s], -1)
                targets = jnp.where(lane == s * slots + k, row, targets)
            return targets

        put(part, lax.fori_loop(0, per, dest, jnp.full((SUBS, LANES), -1, I32)))
    targets = jnp.full((SUBS, LANES), -1, I32)
    for at in range(2 * hubs * chunks):
        targets = jnp.where(lane == at, hub_rows[at % hubs], targets)
    put(n * slots // LANES, targets)
    last = start(spread, spread_out, sems.at[1])
    sent.wait()
    last.wait()


def near_backward(n, slots, hubs, tile_rows, plan, send_rows, send_count, hub_rows, tiles, grad_agg):
    rows, width = grad_agg.shape
    table = n * slots + LANES
    return pl.pallas_call(
        functools.partial(near_backward_kernel, n, slots, hubs),
        out_shape=(pltpu.HBM((rows, width), F32), pltpu.HBM((rows, table), BF16)),
        in_specs=[HBM] * 5 + [VMEM, HBM],
        out_specs=(HBM, HBM),
        scratch_shapes=[
            pltpu.SMEM(tile_rows.shape, I32),
            pltpu.SMEM((PLAN,), I32),
            pltpu.SMEM(send_rows.shape, I32),
            pltpu.SMEM(send_count.shape, I32),
            pltpu.SMEM(hub_rows.shape, I32),
            pltpu.VMEM((rows, width), BF16),
            pltpu.VMEM((rows, width), F32),
            pltpu.VMEM((rows, table), BF16),
            DMA((6,)),
        ],
        compiler_params=params(20 << 20),
        cost_estimate=cost(4 << 30, 8 << 20),
        name="near_backward",
    )(*in_hbm(tile_rows, plan, send_rows, send_count, hub_rows), tiles, *in_hbm(grad_agg))


def collect_kernel(n, slots, hubs, near_in, spread_in, returned, out, near, spread, table, staged, near_sems, spread_sems, out_sems):
    rows, width = near.shape
    chunks = width // LANES
    step = 256
    pieces = [pl.ds(at, step) for at in range(0, rows, step)]
    copies = []
    for b, at in enumerate(pieces):
        copies.append(start(spread_in.at[at], spread.at[at], spread_sems.at[b]))
        copies.append(start(near_in.at[at], near.at[at], near_sems.at[b]))
    unpack_slots(n, slots, chunks, returned, table, 0)
    hub = lax.fori_loop(
        0, n, lambda s, held: held + returned[s, 0:SUBS, :].astype(F32), jnp.zeros((SUBS, LANES), F32), unroll=8
    )
    group = lax.broadcasted_iota(I32, (SUBS, LANES), 0) // hubs
    base = n * slots
    table[base : base + LANES, :] = jnp.zeros((LANES, width), BF16)
    upper = hub.astype(BF16).astype(F32)
    for at, part in ((0, upper), (SUBS, hub - upper)):
        for c in range(chunks):
            table[base + at : base + at + SUBS, c * LANES : (c + 1) * LANES] = jnp.where(
                group == c, part, 0.0
            ).astype(BF16)
    sent = []
    for b, at in enumerate(pieces):
        copies[2 * b].wait()
        more = jnp.dot(spread[at, :], table[...], preferred_element_type=F32)
        copies[2 * b + 1].wait()
        staged[at, :] = (near[at, :] + more).astype(BF16)
        sent.append(start(staged.at[at], out.at[at], out_sems.at[b]))
    for copy in sent:
        copy.wait()


def collect(n, slots, hubs, near, spread, returned):
    rows, width = near.shape
    table = n * slots + LANES
    steps = rows // 256
    return pl.pallas_call(
        functools.partial(collect_kernel, n, slots, hubs),
        out_shape=pltpu.HBM((rows, width), BF16),
        in_specs=[HBM, HBM, VMEM],
        out_specs=HBM,
        scratch_shapes=[
            pltpu.VMEM((rows, width), F32),
            pltpu.VMEM((rows, table), BF16),
            pltpu.VMEM((table, width), BF16),
            pltpu.VMEM((rows, width), BF16),
            DMA((steps,)),
            DMA((steps,)),
            DMA((steps,)),
        ],
        compiler_params=params(20 << 20),
        cost_estimate=cost(2 << 30, 8 << 20),
        name="collect",
    )(*in_hbm(near, spread), returned)


def order_kernel(bits, first, second, out):
    width = out.shape[0]
    unit = width >> bits
    half = 1 << (bits - 1)
    mine = reversed_bits(lax.axis_index("dom"), bits)
    for b in range(half):
        spot = slice(b * unit, (b + 1) * unit)
        out[rows_at(mine ^ b, unit), :] = first[spot, :].astype(F32)
        out[rows_at(mine ^ (b + half), unit), :] = second[spot, :].astype(F32)


def exchange(x, n, bit):
    return lax.ppermute(x, "dom", [(i, i ^ (1 << bit)) for i in range(n)])


def sum_weight(n, keep, give):
    width = keep.shape[1]
    bits = halvings(n, width)
    for bit in range(bits):
        keep = keep + exchange(give, n, bit).astype(F32)
        if bit + 1 < bits:
            half = keep.shape[0] // 2
            keep, give = keep[:half], keep[half:].astype(BF16)
    for bit in range(bits, n.bit_length() - 1):
        keep = keep + exchange(keep.astype(BF16), n, bit).astype(F32)
    held = keep.astype(BF16)
    for bit in reversed(range(1, bits)):
        held = jnp.concatenate([held, exchange(held, n, bit)], axis=0)
    return pl.pallas_call(
        functools.partial(order_kernel, bits),
        out_shape=jax.ShapeDtypeStruct((width, width), F32),
        in_specs=[VMEM, VMEM],
        out_specs=VMEM,
        compiler_params=params(4 << 20),
        name="order",
    )(held, exchange(held, n, 0))


def all_to_all(x):
    return lax.all_to_all(x, "dom", split_axis=0, concat_axis=0, tiled=True)


def per_device(
    features, weight, cotangent, tile_values, tile_rows, tile_cols, hub_rows, send_rows, send_count
):
    n = lax.axis_size("dom")
    slots, hubs = send_rows.shape[2], hub_rows.shape[0]
    send_rows = jnp.swapaxes(send_rows, 1, 2)

    packed = pack_rows(n, send_rows, send_count, hub_rows, features)
    received = all_to_all(packed)
    near, plan = near_forward(tile_rows, tile_cols, tile_values, features)
    output, grad_pre, keep, give = forward(
        n, slots, hubs, tile_rows, tile_cols, plan, tile_values, received, near, weight, cotangent
    )
    far, grad_agg = far_backward(n, slots, hubs, tile_rows, plan, tile_values, grad_pre, weight)
    returned = all_to_all(far)
    near_grad, spread = near_backward(
        n, slots, hubs, tile_rows, plan, send_rows, send_count, hub_rows, tile_values, grad_agg
    )
    grad_features = collect(n, slots, hubs, near_grad, spread, returned)
    grad_weight = sum_weight(n, keep, give)
    return (output, grad_features, grad_weight)


def solution(mesh):
    placed = (
        P("dom", None),
        P(),
        P("dom", None),
        P("dom", None, None),
        P("dom"),
        P("dom"),
        P("dom"),
        P("dom", None, None),
        P("dom", None),
    )
    return jax.shard_map(
        per_device,
        mesh=mesh,
        in_specs=placed,
        out_specs=(P("dom", None), P("dom", None), P()),
        check_vma=False,
    )
```

```python
import functools

import jax
import jax.numpy as jnp
from jax import lax
from jax.experimental import pallas as pl
from jax.experimental.pallas import tpu as pltpu
from jax.sharding import PartitionSpec as P

LOC_TILES = 64
LANES = 128
SUBS = 16
NONE = 255
KEYS = 32
LIST = 64
UNROLL = 4
HALVED = (0, 3, 4)
NEAR_FWD, FAR_FWD, NEAR_BWD, FAR_BWD = range(4)
COUNTS = 4 * LIST
PLAN = COUNTS + LANES
VMEM = pl.BlockSpec(memory_space=pltpu.VMEM)
HBM = pl.BlockSpec(memory_space=pltpu.HBM)
DMA = pltpu.SemaphoreType.DMA
BF16, F32, I32 = jnp.bfloat16, jnp.float32, jnp.int32


def rows_at(block, size):
    return pl.ds(pl.multiple_of(block * size, size), size)


def params(limit):
    return pltpu.CompilerParams(vmem_limit_bytes=limit)


def in_hbm(*arrays):
    return [pltpu.with_memory_space_constraint(a, pltpu.HBM) for a in arrays]


def in_vmem(*arrays):
    return [pltpu.with_memory_space_constraint(a, pltpu.VMEM) for a in arrays]


def cost(flops, moved):
    return pl.CostEstimate(flops=flops, bytes_accessed=moved, transcendentals=0)


def start(source, target, sem):
    copy = pltpu.make_async_copy(source, target, sem)
    copy.start()
    return copy


def pack_kernel(
    n, slots, hubs, send_rows_in, send_count_in, hub_rows_in, feats_in, out,
    send_rows, send_count, hub_rows, feats, select, staged, sems, out_sems,
):
    rows, width = feats.shape
    chunks = width // LANES
    copies = [
        start(a, b, sems.at[i])
        for i, (a, b) in enumerate(
            (
                (send_rows_in, send_rows),
                (send_count_in, send_count),
                (hub_rows_in, hub_rows),
                (feats_in, feats),
            )
        )
    ]
    sub = lax.broadcasted_iota(I32, (2 * slots, LANES), 0)
    lane = lax.broadcasted_iota(I32, (2 * slots, LANES), 1)
    for copy in copies[:3]:
        copy.wait()

    def put(at, column):
        for part in range(rows // LANES):
            hit = jnp.where(column == lane + part * LANES, 1.0, 0.0)
            select[rows_at(at, 2 * slots), part * LANES : (part + 1) * LANES] = hit.astype(BF16)

    column = jnp.zeros((2 * slots, LANES), I32)
    for row in range(hubs * chunks):
        column = jnp.where(sub == row, hub_rows[row % hubs], column)
    put(0, column)

    def pair(q, _):
        column = jnp.full((2 * slots, LANES), -1, I32)
        for half in range(2):
            dest = 2 * q + half
            count = send_count[0, dest]
            for k in range(slots):
                row = jnp.where(k < count, send_rows[0, k, dest], -1)
                column = jnp.where(sub == half * slots + k, row, column)
        put(q + 1, column)
        return 0

    lax.fori_loop(0, n // 2, pair, 0, unroll=2)
    copies[3].wait()
    group = sub // hubs
    found = jnp.dot(select[0 : 2 * slots, :], feats[...], preferred_element_type=F32)
    hub = jnp.zeros((hubs * chunks, LANES), F32)
    for c in range(chunks):
        hub = jnp.where(group == c, found[:, c * LANES : (c + 1) * LANES], hub)
    hub = hub.astype(BF16)
    per = LANES // slots
    sent = []
    for b in range(n // per):
        got = jnp.dot(
            select[b * LANES + 2 * slots : (b + 1) * LANES + 2 * slots, :], feats[...], preferred_element_type=F32
        )
        for s in range(per):
            dest = b * per + s
            staged[dest, 0:SUBS, :] = hub
            mine = got[s * slots : (s + 1) * slots, :]
            for c in range(0, chunks, 2):
                both = jnp.concatenate(
                    [mine[:, c * LANES : (c + 1) * LANES], mine[:, (c + 1) * LANES : (c + 2) * LANES]], axis=0
                )
                staged[dest, SUBS + c * slots : SUBS + (c + 2) * slots, :] = both.astype(BF16)
        group_of = pl.ds(b * per, per)
        sent.append(start(staged.at[group_of], out.at[group_of], out_sems.at[b]))
    for copy in sent:
        copy.wait()


def pack_rows(n, send_rows, send_count, hub_rows, features):
    slots, hubs = send_rows.shape[1], hub_rows.shape[0]
    rows, width = features.shape
    packed = (n, (slots + hubs) * width // LANES, LANES)
    return pl.pallas_call(
        functools.partial(pack_kernel, n, slots, hubs),
        out_shape=pltpu.HBM(packed, BF16),
        in_specs=[HBM] * 4,
        out_specs=HBM,
        scratch_shapes=[
            pltpu.SMEM(send_rows.shape, I32),
            pltpu.SMEM(send_count.shape, I32),
            pltpu.SMEM(hub_rows.shape, I32),
            pltpu.VMEM((rows, width), BF16),
            pltpu.VMEM((n * slots + 2 * slots, rows), BF16),
            pltpu.VMEM(packed, BF16),
            DMA((4,)),
            DMA((n * slots // LANES,)),
        ],
        compiler_params=params(16 << 20),
        name="pack_rows",
    )(*in_hbm(send_rows, send_count, hub_rows, features))


def make_plan(tile_rows, tile_cols, blocks, plan, waiting):
    def clear(i, _):
        waiting[i] = NONE
        return 0

    lax.fori_loop(0, 4 * KEYS, clear, 0, unroll=8)
    for kind in range(4):
        plan[COUNTS + kind] = 0

    def add(kind, key, t):
        slot = kind * KEYS + key
        first, count = waiting[slot], plan[COUNTS + kind]
        pair = first != NONE
        plan[kind * LIST + count] = (key << 16) | (first << 8) | t
        plan[COUNTS + kind] = count + pair.astype(I32)
        waiting[slot] = jnp.where(pair, NONE, t)

    def tile(t, _):
        row, col = tile_rows[t], tile_cols[t]
        far = (col >= blocks).astype(I32)
        add(NEAR_FWD + far, row, t)
        add(NEAR_BWD + far, col - blocks * far, t)
        return 0

    lax.fori_loop(0, tile_rows.shape[0], tile, 0)
    for kind in range(4):

        def left(key, count, kind=kind):
            first = waiting[kind * KEYS + key]
            plan[kind * LIST + count] = (key << 16) | (first << 8) | NONE
            return count + (first != NONE).astype(I32)

        count = lax.fori_loop(0, KEYS, left, plan[COUNTS + kind])
        plan[COUNTS + kind] = count
        for u in range(UNROLL):
            plan[kind * LIST + count + u] = (NONE << 8) | NONE


def run_plan(kind, plan, tiles, source_of, source, total, transposed):
    size, last = tiles.shape[1], tiles.shape[0] - 1
    axis = 0 if transposed else 1

    def group(g, _):
        for u in range(UNROLL):
            word = plan[kind * LIST + g * UNROLL + u]
            key, picks = word >> 16, ((word >> 8) & 255, word & 255)
            left, right = [], []
            for pick in picks:
                t = jnp.minimum(pick, last)
                left.append(jnp.where(pick == NONE, jnp.zeros((size, size), BF16), tiles[t]))
                right.append(source[rows_at(source_of(t), size), :])
            total[rows_at(key, size), :] += lax.dot_general(
                jnp.concatenate(left, axis=axis),
                jnp.concatenate(right, axis=0),
                (((axis,), (0,)), ((), ())),
                preferred_element_type=F32,
            )
        return 0

    lax.fori_loop(0, (plan[COUNTS + kind] + UNROLL - 1) // UNROLL, group, 0)


def make_spread(n, slots, hubs, chunks, send_rows, send_count, hub_rows, spread):
    rows = spread.shape[0]
    lane = lax.broadcasted_iota(I32, (SUBS, LANES), 1)
    sub = lax.broadcasted_iota(I32, (SUBS, LANES), 0)

    def put(part, targets):
        def rows_of(b, _):
            hit = jnp.where(targets == sub + b * SUBS, 1.0, 0.0)
            spread[rows_at(b, SUBS), part * LANES : (part + 1) * LANES] = hit.astype(BF16)
            return 0

        lax.fori_loop(0, rows // SUBS, rows_of, 0, unroll=8)

    per = LANES // slots
    for part in range(n * slots // LANES):

        def dest(s, targets, part=part):
            count = send_count[0, part * per + s]
            for k in range(slots):
                row = jnp.where(k < count, send_rows[0, k, part * per + s], -1)
                targets = jnp.where(lane == s * slots + k, row, targets)
            return targets

        put(part, lax.fori_loop(0, per, dest, jnp.full((SUBS, LANES), -1, I32)))
    targets = jnp.full((SUBS, LANES), -1, I32)
    for at in range(2 * hubs * chunks):
        targets = jnp.where(lane == at, hub_rows[at % hubs], targets)
    put(n * slots // LANES, targets)


def near_forward_kernel(
    n, slots, hubs, tile_rows_in, tile_cols_in, send_rows_in, send_count_in, hub_rows_in, tiles, feats_in,
    near_out, plan_out, spread_out,
    tile_rows, tile_cols, send_rows, send_count, hub_rows, feats, total, spread, plan, waiting, sems,
):
    rows, width = feats.shape
    blocks = rows // tiles.shape[1]
    moves = (
        (tile_rows_in, tile_rows),
        (tile_cols_in, tile_cols),
        (send_rows_in, send_rows),
        (send_count_in, send_count),
        (hub_rows_in, hub_rows),
        (feats_in, feats),
    )
    copies = [start(a, b, sems.at[i]) for i, (a, b) in enumerate(moves)]
    total[...] = jnp.zeros_like(total)
    copies[0].wait()
    copies[1].wait()
    make_plan(tile_rows, tile_cols, blocks, plan, waiting)
    sent = [start(plan, plan_out, sems.at[0])]
    for copy in copies[2:]:
        copy.wait()
    run_plan(NEAR_FWD, plan, tiles, lambda t: jnp.minimum(tile_cols[t], blocks - 1), feats, total, False)
    sent.append(start(total, near_out, sems.at[1]))
    make_spread(n, slots, hubs, width // LANES, send_rows, send_count, hub_rows, spread)
    sent.append(start(spread, spread_out, sems.at[2]))
    for copy in sent:
        copy.wait()


def near_forward(n, tile_rows, tile_cols, send_rows, send_count, hub_rows, tiles, features):
    rows, width = features.shape
    slots, hubs = send_rows.shape[1], hub_rows.shape[0]
    return pl.pallas_call(
        functools.partial(near_forward_kernel, n, slots, hubs),
        out_shape=(
            pltpu.HBM((rows, width), F32),
            pltpu.HBM((PLAN,), I32),
            pltpu.HBM((rows, n * slots + LANES), BF16),
        ),
        in_specs=[HBM] * 5 + [VMEM, HBM],
        out_specs=(HBM, HBM, HBM),
        scratch_shapes=[
            pltpu.SMEM(tile_rows.shape, I32),
            pltpu.SMEM(tile_cols.shape, I32),
            pltpu.SMEM(send_rows.shape, I32),
            pltpu.SMEM(send_count.shape, I32),
            pltpu.SMEM(hub_rows.shape, I32),
            pltpu.VMEM((rows, width), BF16),
            pltpu.VMEM((rows, width), F32),
            pltpu.VMEM((rows, n * slots + LANES), BF16),
            pltpu.SMEM((PLAN,), I32),
            pltpu.SMEM((4 * KEYS,), I32),
            DMA((6,)),
        ],
        compiler_params=params(20 << 20),
        cost_estimate=cost(4 << 30, 8 << 20),
        name="near_forward",
    )(
        *in_hbm(tile_rows, tile_cols, send_rows, send_count, hub_rows),
        *in_vmem(tiles),
        *in_hbm(features),
    )


def unpack_slots(n, slots, chunks, packed, into, at):
    def pair(q, _):
        for c in range(0, chunks, 2):
            spot = slice(SUBS + c * slots, SUBS + (c + 2) * slots)
            first = packed[2 * q, spot, :].astype(F32)
            second = packed[2 * q + 1, spot, :].astype(F32)
            for half in range(2):
                part = slice(half * slots, (half + 1) * slots)
                both = jnp.concatenate([first[part], second[part]], axis=0).astype(BF16)
                where = pl.ds(pl.multiple_of(at + q * 2 * slots, 2 * slots), 2 * slots)
                into[where, (c + half) * LANES : (c + half + 1) * LANES] = both
        return 0

    lax.fori_loop(0, n // 2, pair, 0, unroll=4)


def place():
    device = lax.axis_index("dom")
    out = jnp.zeros((), I32)
    for at, bit in enumerate(HALVED):
        out = out | (((device >> bit) & 1) << (len(HALVED) - 1 - at))
    return out


def forward_kernel(
    n, slots, hubs, tile_rows_in, tile_cols_in, plan_in, tiles, received, near_in, weight_in, cot_in,
    output, grad_agg_out, keep, give,
    tile_rows, tile_cols, plan, table, total, near, weight, cot, agg, grad_pre, grad_agg, out, sems, near_sems, cot_sems, out_sems, ga_sems,
):
    size = tiles.shape[1]
    rows, width = near.shape
    chunks = width // LANES
    blocks = rows // size
    step = 256
    steps = rows // step
    index = [
        start(a, b, sems.at[i])
        for i, (a, b) in enumerate(((plan_in, plan), (tile_rows_in, tile_rows), (tile_cols_in, tile_cols)))
    ]
    weight_copy = start(weight_in, weight, sems.at[3])
    pieces = [pl.ds(b * step, step) for b in range(steps)]
    arrivals = [
        (start(near_in.at[at], near.at[at], near_sems.at[b]), start(cot_in.at[at], cot.at[at], cot_sems.at[b]))
        for b, at in enumerate(pieces)
    ]
    total[...] = jnp.zeros_like(total)

    def four(q, _):
        parts = [received[4 * q + u, 0:SUBS, :].astype(F32) for u in range(4)]
        for c in range(chunks):
            quad = jnp.concatenate([part[c * hubs : (c + 1) * hubs] for part in parts], axis=0)
            table[rows_at(q, SUBS), c * LANES : (c + 1) * LANES] = quad.astype(BF16)
        return 0

    lax.fori_loop(0, n // 4, four, 0, unroll=2)
    unpack_slots(n, slots, chunks, received, table, n * hubs)
    for copy in index:
        copy.wait()
    run_plan(FAR_FWD, plan, tiles, lambda t: jnp.maximum(tile_cols[t] - blocks, 0), table, total, False)
    weight_copy.wait()
    for pair in arrivals:
        for copy in pair:
            copy.wait()

    def first(at):
        here = (total[at, :] + near[at, :]).astype(BF16)
        agg[at, :] = here
        return jnp.dot(here, weight[...], preferred_element_type=F32)

    sent = []
    pre = first(pieces[0])
    for b, at in enumerate(pieces):
        following = first(pieces[b + 1]) if b + 1 < steps else None
        sig = 0.5 * jnp.tanh(0.5 * pre) + 0.5
        out[at, :] = (pre * sig).astype(BF16)
        gp = (cot[at, :].astype(F32) * sig * (1.0 + pre * (1.0 - sig))).astype(BF16)
        grad_pre[at, :] = gp
        grad_agg[at, :] = lax.dot_general(
            gp, weight[...], (((1,), (1,)), ((), ())), preferred_element_type=F32
        ).astype(BF16)
        sent.append(start(out.at[at], output.at[at], out_sems.at[b]))
        sent.append(start(grad_agg.at[at], grad_agg_out.at[at], ga_sems.at[b]))
        pre = following
    scale = float(rows * n) ** -0.5
    term = total.at[pl.ds(0, width)]
    for c in range(0, width, 256):
        term[c : c + 256, :] = (
            lax.dot_general(
                agg[:, c : c + 256], grad_pre[...], (((0,), (0,)), ((), ())), preferred_element_type=F32
            )
            * scale
        )
    half = 1 << (len(HALVED) - 1)
    unit = width // (2 * half)
    mine = place()
    for b in range(half):
        spot = slice(b * unit, (b + 1) * unit)
        keep[spot, :] = term[rows_at(mine ^ b, unit), :]
        give[spot, :] = term[rows_at(mine ^ (b + half), unit), :].astype(BF16)
    for copy in sent:
        copy.wait()


def forward(n, slots, hubs, tile_rows, tile_cols, plan, tiles, received, near, weight, cotangent):
    rows, width = near.shape
    steps = rows // 256
    return pl.pallas_call(
        functools.partial(forward_kernel, n, slots, hubs),
        out_shape=(
            pltpu.HBM((rows, width), BF16),
            pltpu.HBM((rows, width), BF16),
            pltpu.VMEM((width // 2, width), F32),
            pltpu.VMEM((width // 2, width), BF16),
        ),
        in_specs=[HBM, HBM, HBM, VMEM, VMEM, HBM, HBM, HBM],
        out_specs=(HBM, HBM, VMEM, VMEM),
        scratch_shapes=[
            pltpu.SMEM(tile_rows.shape, I32),
            pltpu.SMEM(tile_cols.shape, I32),
            pltpu.SMEM((PLAN,), I32),
            pltpu.VMEM((n * (slots + hubs), width), BF16),
            pltpu.VMEM((rows, width), F32),
            pltpu.VMEM((rows, width), F32),
            pltpu.VMEM((width, width), BF16),
            pltpu.VMEM((rows, width), BF16),
            pltpu.VMEM((rows, width), BF16),
            pltpu.VMEM((rows, width), BF16),
            pltpu.VMEM((rows, width), BF16),
            pltpu.VMEM((rows, width), BF16),
            DMA((4,)),
            DMA((steps,)),
            DMA((steps,)),
            DMA((steps,)),
            DMA((steps,)),
        ],
        compiler_params=params(28 << 20),
        cost_estimate=cost(8 << 30, 16 << 20),
        name="forward",
    )(*in_hbm(tile_rows, tile_cols, plan), *in_vmem(tiles, received), *in_hbm(near, weight, cotangent))


def far_backward_kernel(
    n, slots, hubs, tile_rows_in, plan_in, tiles, grad_agg_in, out, tile_rows, plan, grad_agg, total, staged, sems
):
    chunks = grad_agg.shape[1] // LANES
    moves = ((plan_in, plan), (tile_rows_in, tile_rows), (grad_agg_in, grad_agg))
    copies = [start(a, b, sems.at[i]) for i, (a, b) in enumerate(moves)]
    total[...] = jnp.zeros_like(total)
    for copy in copies:
        copy.wait()
    run_plan(FAR_BWD, plan, tiles, lambda t: tile_rows[t], grad_agg, total, True)

    def two(q, _):
        both = total[rows_at(q, 2 * hubs), :]
        for u in range(2):
            mine = both[u * hubs : (u + 1) * hubs]
            staged[2 * q + u, 0:SUBS, :] = jnp.concatenate(
                [mine[:, c * LANES : (c + 1) * LANES] for c in range(chunks)], axis=0
            ).astype(BF16)
            halo = total[pl.ds(pl.multiple_of(n * hubs + (2 * q + u) * slots, slots), slots), :]
            for c in range(0, chunks, 2):
                pair = jnp.concatenate(
                    [halo[:, c * LANES : (c + 1) * LANES], halo[:, (c + 1) * LANES : (c + 2) * LANES]], axis=0
                )
                staged[2 * q + u, SUBS + c * slots : SUBS + (c + 2) * slots, :] = pair.astype(BF16)
        return 0

    lax.fori_loop(0, n // 2, two, 0, unroll=2)
    start(staged, out, sems.at[0]).wait()


def far_backward(n, slots, hubs, tile_rows, plan, tiles, grad_agg):
    width = grad_agg.shape[1]
    packed = (n, (slots + hubs) * width // LANES, LANES)
    return pl.pallas_call(
        functools.partial(far_backward_kernel, n, slots, hubs),
        out_shape=pltpu.HBM(packed, BF16),
        in_specs=[HBM, HBM, VMEM, HBM],
        out_specs=HBM,
        scratch_shapes=[
            pltpu.SMEM(tile_rows.shape, I32),
            pltpu.SMEM((PLAN,), I32),
            pltpu.VMEM(grad_agg.shape, BF16),
            pltpu.VMEM((n * (slots + hubs), width), F32),
            pltpu.VMEM(packed, BF16),
            DMA((3,)),
        ],
        compiler_params=params(12 << 20),
        cost_estimate=cost(4 << 30, 8 << 20),
        name="far_backward",
    )(*in_hbm(tile_rows, plan), *in_vmem(tiles), *in_hbm(grad_agg))


def near_backward_kernel(
    tile_rows_in, plan_in, tiles_in, grad_agg_in, out, tile_rows, plan, tiles, grad_agg, total, sems
):
    near = tiles_in.at[pl.ds(0, LOC_TILES)]
    moves = ((tile_rows_in, tile_rows), (plan_in, plan), (grad_agg_in, grad_agg), (near, tiles))
    copies = [start(a, b, sems.at[i]) for i, (a, b) in enumerate(moves)]
    total[...] = jnp.zeros_like(total)
    for copy in copies:
        copy.wait()
    run_plan(NEAR_BWD, plan, tiles, lambda t: tile_rows[t], grad_agg, total, True)
    out[...] = total[...].astype(BF16)


def near_backward(tile_rows, plan, tiles, grad_agg):
    return pl.pallas_call(
        near_backward_kernel,
        out_shape=pltpu.VMEM(grad_agg.shape, BF16),
        in_specs=[HBM] * 4,
        out_specs=VMEM,
        scratch_shapes=[
            pltpu.SMEM(tile_rows.shape, I32),
            pltpu.SMEM((PLAN,), I32),
            pltpu.VMEM((LOC_TILES,) + tiles.shape[1:], BF16),
            pltpu.VMEM(grad_agg.shape, BF16),
            pltpu.VMEM(grad_agg.shape, F32),
            DMA((4,)),
        ],
        compiler_params=params(16 << 20),
        cost_estimate=cost(4 << 30, 8 << 20),
        name="near_backward",
    )(*in_hbm(tile_rows, plan, tiles, grad_agg))


def collect_kernel(
    n, slots, hubs, near, spread_in, returned, out, spread, table, staged, spread_sems, out_sems
):
    rows, width = staged.shape
    chunks = width // LANES
    step = 256
    pieces = [pl.ds(at, step) for at in range(0, rows, step)]
    arrival = start(spread_in, spread, spread_sems.at[0])
    unpack_slots(n, slots, chunks, returned, table, 0)
    hub = lax.fori_loop(
        0, n, lambda s, held: held + returned[s, 0:SUBS, :].astype(F32), jnp.zeros((SUBS, LANES), F32), unroll=8
    )
    group = lax.broadcasted_iota(I32, (SUBS, LANES), 0) // hubs
    base = n * slots
    table[base : base + LANES, :] = jnp.zeros((LANES, width), BF16)
    upper = hub.astype(BF16).astype(F32)
    for at, part in ((0, upper), (SUBS, hub - upper)):
        for c in range(chunks):
            table[base + at : base + at + SUBS, c * LANES : (c + 1) * LANES] = jnp.where(
                group == c, part, 0.0
            ).astype(BF16)
    sent = []
    arrival.wait()
    for b, at in enumerate(pieces):
        more = jnp.dot(spread[at, :], table[...], preferred_element_type=F32)
        staged[at, :] = (near[at, :].astype(F32) + more).astype(BF16)
        sent.append(start(staged.at[at], out.at[at], out_sems.at[b]))
    for copy in sent:
        copy.wait()


def collect(n, slots, hubs, near, spread, returned):
    rows, width = near.shape
    table = n * slots + LANES
    return pl.pallas_call(
        functools.partial(collect_kernel, n, slots, hubs),
        out_shape=pltpu.HBM((rows, width), BF16),
        in_specs=[VMEM, HBM, VMEM],
        out_specs=HBM,
        scratch_shapes=[
            pltpu.VMEM((rows, table), BF16),
            pltpu.VMEM((table, width), BF16),
            pltpu.VMEM((rows, width), BF16),
            DMA((1,)),
            DMA((rows // 256,)),
        ],
        compiler_params=params(16 << 20),
        cost_estimate=cost(32 << 30, 8 << 20),
        name="collect",
    )(*in_vmem(near), *in_hbm(spread), *in_vmem(returned))


def order_kernel(first, second, out):
    half = 1 << (len(HALVED) - 1)
    unit = out.shape[0] // (2 * half)
    mine = place()
    for b in range(half):
        spot = slice(b * unit, (b + 1) * unit)
        out[rows_at(mine ^ b, unit), :] = first[spot, :].astype(F32)
        out[rows_at(mine ^ (b + half), unit), :] = second[spot, :].astype(F32)


def exchange(x, n, bit):
    return lax.ppermute(x, "dom", [(i, i ^ (1 << bit)) for i in range(n)])


def tie(*arrays):
    return lax.optimization_barrier(arrays)


def all_to_all(x):
    return lax.all_to_all(x, "dom", split_axis=0, concat_axis=0, tiled=True)


def per_device(
    features, weight, cotangent, tile_values, tile_rows, tile_cols, hub_rows, send_rows, send_count
):
    n = lax.axis_size("dom")
    slots, hubs = send_rows.shape[2], hub_rows.shape[0]
    send_rows = jnp.swapaxes(send_rows, 1, 2)

    packed = pack_rows(n, send_rows, send_count, hub_rows, features)
    received = all_to_all(packed)
    near, plan, spread = near_forward(
        n, tile_rows, tile_cols, send_rows, send_count, hub_rows, tile_values, features
    )
    output, grad_agg, keep, give = forward(
        n, slots, hubs, tile_rows, tile_cols, plan, tile_values, received, near, weight, cotangent
    )
    width = keep.shape[1]
    keep = keep + exchange(give, n, HALVED[0]).astype(F32)
    half = keep.shape[0] // 2
    keep, give, grad_agg = tie(keep[:half].astype(BF16), keep[half:].astype(BF16), grad_agg)
    got = exchange(give, n, HALVED[1])
    far = far_backward(n, slots, hubs, tile_rows, plan, tile_values, grad_agg)
    half = half // 2
    give = (keep[half:].astype(F32) + got[half:].astype(F32)).astype(BF16)
    keep = (keep[:half].astype(F32) + got[:half].astype(F32)).astype(BF16)
    keep, give, far = tie(keep, give, far)
    got = exchange(give, n, HALVED[2])
    returned = all_to_all(far)
    held, grad_agg = tie((keep.astype(F32) + got.astype(F32)).astype(BF16), grad_agg)
    for bit in range(n.bit_length() - 1):
        if bit not in HALVED:
            got = exchange(held, n, bit)
            if bit == 2:
                near_grad = near_backward(tile_rows, plan, tile_values, grad_agg)
            held, grad_agg = tie((held.astype(F32) + got.astype(F32)).astype(BF16), grad_agg)
    held, near_grad = tie(held, near_grad)
    got = exchange(held, n, HALVED[2])
    held, returned = tie(jnp.concatenate([held, got], axis=0), returned)
    got = exchange(held, n, HALVED[1])
    grad_features = collect(n, slots, hubs, near_grad, spread, returned)
    held, grad_features = tie(jnp.concatenate([held, got], axis=0), grad_features)
    grad_weight = pl.pallas_call(
        order_kernel,
        out_shape=jax.ShapeDtypeStruct((width, width), F32),
        in_specs=[VMEM, VMEM],
        out_specs=VMEM,
        compiler_params=params(4 << 20),
        name="order",
    )(held, exchange(held, n, HALVED[0]))
    return (output, grad_features, grad_weight)


def solution(mesh):
    placed = (
        P("dom", None),
        P(),
        P("dom", None),
        P("dom", None, None),
        P("dom"),
        P("dom"),
        P("dom"),
        P("dom", None, None),
        P("dom", None),
    )
    return jax.shard_map(
        per_device,
        mesh=mesh,
        in_specs=placed,
        out_specs=(P("dom", None), P("dom", None), P()),
        check_vma=False,
    )
```

```python
import functools

import jax
import jax.numpy as jnp
from jax import lax
from jax.experimental import pallas as pl
from jax.experimental.pallas import tpu as pltpu
from jax.sharding import PartitionSpec as P

LOC_TILES = 64
LANES = 128
SUBS = 16
NONE = 255
KEYS = 32
LIST = 64
UNROLL = 4
HALVED = (0, 3, 4)
NEAR_FWD, FAR_FWD, NEAR_BWD, FAR_BWD = range(4)
COUNTS = 4 * LIST
PLAN = COUNTS + LANES
VMEM = pl.BlockSpec(memory_space=pltpu.VMEM)
HBM = pl.BlockSpec(memory_space=pltpu.HBM)
DMA = pltpu.SemaphoreType.DMA
BF16, F32, I32 = jnp.bfloat16, jnp.float32, jnp.int32


def rows_at(block, size):
    return pl.ds(pl.multiple_of(block * size, size), size)


def params(limit):
    return pltpu.CompilerParams(vmem_limit_bytes=limit)


def in_hbm(*arrays):
    return [pltpu.with_memory_space_constraint(a, pltpu.HBM) for a in arrays]


def in_vmem(*arrays):
    return [pltpu.with_memory_space_constraint(a, pltpu.VMEM) for a in arrays]


def cost(flops, moved):
    return pl.CostEstimate(flops=flops, bytes_accessed=moved, transcendentals=0)


def start(source, target, sem):
    copy = pltpu.make_async_copy(source, target, sem)
    copy.start()
    return copy


def pack_kernel(
    n, slots, hubs, send_rows_in, send_count_in, hub_rows_in, feats_in, out,
    send_rows, send_count, hub_rows, feats, select, staged, sems, out_sems,
):
    rows, width = feats.shape
    chunks = width // LANES
    copies = [
        start(a, b, sems.at[i])
        for i, (a, b) in enumerate(
            (
                (send_rows_in, send_rows),
                (send_count_in, send_count),
                (hub_rows_in, hub_rows),
                (feats_in, feats),
            )
        )
    ]
    sub = lax.broadcasted_iota(I32, (2 * slots, LANES), 0)
    lane = lax.broadcasted_iota(I32, (2 * slots, LANES), 1)
    for copy in copies[:3]:
        copy.wait()

    def put(at, column):
        for part in range(rows // LANES):
            hit = jnp.where(column == lane + part * LANES, 1.0, 0.0)
            select[rows_at(at, 2 * slots), part * LANES : (part + 1) * LANES] = hit.astype(BF16)

    column = jnp.zeros((2 * slots, LANES), I32)
    for row in range(hubs * chunks):
        column = jnp.where(sub == row, hub_rows[row % hubs], column)
    put(0, column)

    def pair(q, _):
        column = jnp.full((2 * slots, LANES), -1, I32)
        for half in range(2):
            dest = 2 * q + half
            count = send_count[0, dest]
            for k in range(slots):
                row = jnp.where(k < count, send_rows[0, k, dest], -1)
                column = jnp.where(sub == half * slots + k, row, column)
        put(q + 1, column)
        return 0

    lax.fori_loop(0, n // 2, pair, 0, unroll=2)
    copies[3].wait()
    group = sub // hubs
    found = jnp.dot(select[0 : 2 * slots, :], feats[...], preferred_element_type=F32)
    hub = jnp.zeros((hubs * chunks, LANES), F32)
    for c in range(chunks):
        hub = jnp.where(group == c, found[:, c * LANES : (c + 1) * LANES], hub)
    hub = hub.astype(BF16)
    per = LANES // slots
    sent = []
    for b in range(n // per):
        got = jnp.dot(
            select[b * LANES + 2 * slots : (b + 1) * LANES + 2 * slots, :], feats[...], preferred_element_type=F32
        )
        for s in range(per):
            dest = b * per + s
            staged[dest, 0:SUBS, :] = hub
            mine = got[s * slots : (s + 1) * slots, :]
            for c in range(0, chunks, 2):
                both = jnp.concatenate(
                    [mine[:, c * LANES : (c + 1) * LANES], mine[:, (c + 1) * LANES : (c + 2) * LANES]], axis=0
                )
                staged[dest, SUBS + c * slots : SUBS + (c + 2) * slots, :] = both.astype(BF16)
        group_of = pl.ds(b * per, per)
        sent.append(start(staged.at[group_of], out.at[group_of], out_sems.at[b]))
    for copy in sent:
        copy.wait()


def pack_rows(n, send_rows, send_count, hub_rows, features):
    slots, hubs = send_rows.shape[1], hub_rows.shape[0]
    rows, width = features.shape
    packed = (n, (slots + hubs) * width // LANES, LANES)
    return pl.pallas_call(
        functools.partial(pack_kernel, n, slots, hubs),
        out_shape=pltpu.HBM(packed, BF16),
        in_specs=[HBM] * 4,
        out_specs=HBM,
        scratch_shapes=[
            pltpu.SMEM(send_rows.shape, I32),
            pltpu.SMEM(send_count.shape, I32),
            pltpu.SMEM(hub_rows.shape, I32),
            pltpu.VMEM((rows, width), BF16),
            pltpu.VMEM((n * slots + 2 * slots, rows), BF16),
            pltpu.VMEM(packed, BF16),
            DMA((4,)),
            DMA((n * slots // LANES,)),
        ],
        compiler_params=params(16 << 20),
        name="pack_rows",
    )(*in_hbm(send_rows, send_count, hub_rows, features))


def make_plan(tile_rows, tile_cols, blocks, plan, waiting):
    def clear(i, _):
        waiting[i] = NONE
        return 0

    lax.fori_loop(0, 4 * KEYS, clear, 0, unroll=8)
    for kind in range(4):
        plan[COUNTS + kind] = 0

    def add(kind, key, t):
        slot = kind * KEYS + key
        first, count = waiting[slot], plan[COUNTS + kind]
        pair = first != NONE
        plan[kind * LIST + count] = (key << 16) | (first << 8) | t
        plan[COUNTS + kind] = count + pair.astype(I32)
        waiting[slot] = jnp.where(pair, NONE, t)

    def tile(t, _):
        row, col = tile_rows[t], tile_cols[t]
        far = (col >= blocks).astype(I32)
        add(NEAR_FWD + far, row, t)
        add(NEAR_BWD + far, col - blocks * far, t)
        return 0

    lax.fori_loop(0, tile_rows.shape[0], tile, 0)
    for kind in range(4):

        def left(key, count, kind=kind):
            first = waiting[kind * KEYS + key]
            plan[kind * LIST + count] = (key << 16) | (first << 8) | NONE
            return count + (first != NONE).astype(I32)

        count = lax.fori_loop(0, KEYS, left, plan[COUNTS + kind])
        plan[COUNTS + kind] = count
        for u in range(UNROLL):
            plan[kind * LIST + count + u] = (NONE << 8) | NONE


def run_plan(kind, plan, tiles, source_of, source, total, transposed):
    size, last = tiles.shape[1], tiles.shape[0] - 1
    axis = 0 if transposed else 1

    def group(g, _):
        for u in range(UNROLL):
            word = plan[kind * LIST + g * UNROLL + u]
            key, picks = word >> 16, ((word >> 8) & 255, word & 255)
            left, right = [], []
            for pick in picks:
                t = jnp.minimum(pick, last)
                left.append(jnp.where(pick == NONE, jnp.zeros((size, size), BF16), tiles[t]))
                right.append(source[rows_at(source_of(t), size), :])
            total[rows_at(key, size), :] += lax.dot_general(
                jnp.concatenate(left, axis=axis),
                jnp.concatenate(right, axis=0),
                (((axis,), (0,)), ((), ())),
                preferred_element_type=F32,
            )
        return 0

    lax.fori_loop(0, (plan[COUNTS + kind] + UNROLL - 1) // UNROLL, group, 0)


def make_spread(n, slots, hubs, chunks, send_rows, send_count, hub_rows, spread):
    rows = spread.shape[0]
    lane = lax.broadcasted_iota(I32, (SUBS, LANES), 1)
    sub = lax.broadcasted_iota(I32, (SUBS, LANES), 0)

    def put(part, targets):
        def rows_of(b, _):
            hit = jnp.where(targets == sub + b * SUBS, 1.0, 0.0)
            spread[rows_at(b, SUBS), part * LANES : (part + 1) * LANES] = hit.astype(BF16)
            return 0

        lax.fori_loop(0, rows // SUBS, rows_of, 0, unroll=8)

    per = LANES // slots
    for part in range(n * slots // LANES):

        def dest(s, targets, part=part):
            count = send_count[0, part * per + s]
            for k in range(slots):
                row = jnp.where(k < count, send_rows[0, k, part * per + s], -1)
                targets = jnp.where(lane == s * slots + k, row, targets)
            return targets

        put(part, lax.fori_loop(0, per, dest, jnp.full((SUBS, LANES), -1, I32)))
    targets = jnp.full((SUBS, LANES), -1, I32)
    for at in range(2 * hubs * chunks):
        targets = jnp.where(lane == at, hub_rows[at % hubs], targets)
    put(n * slots // LANES, targets)


def near_forward_kernel(
    n, slots, hubs, tile_rows_in, tile_cols_in, send_rows_in, send_count_in, hub_rows_in, tiles, feats_in,
    near_out, plan_out, spread_out,
    tile_rows, tile_cols, send_rows, send_count, hub_rows, feats, total, spread, plan, waiting, sems,
):
    rows, width = feats.shape
    blocks = rows // tiles.shape[1]
    moves = (
        (tile_rows_in, tile_rows),
        (tile_cols_in, tile_cols),
        (send_rows_in, send_rows),
        (send_count_in, send_count),
        (hub_rows_in, hub_rows),
        (feats_in, feats),
    )
    copies = [start(a, b, sems.at[i]) for i, (a, b) in enumerate(moves)]
    total[...] = jnp.zeros_like(total)
    copies[0].wait()
    copies[1].wait()
    make_plan(tile_rows, tile_cols, blocks, plan, waiting)
    sent = [start(plan, plan_out, sems.at[0])]
    for copy in copies[2:]:
        copy.wait()
    run_plan(NEAR_FWD, plan, tiles, lambda t: jnp.minimum(tile_cols[t], blocks - 1), feats, total, False)
    sent.append(start(total, near_out, sems.at[1]))
    make_spread(n, slots, hubs, width // LANES, send_rows, send_count, hub_rows, spread)
    sent.append(start(spread, spread_out, sems.at[2]))
    for copy in sent:
        copy.wait()


def near_forward(n, tile_rows, tile_cols, send_rows, send_count, hub_rows, tiles, features):
    rows, width = features.shape
    slots, hubs = send_rows.shape[1], hub_rows.shape[0]
    return pl.pallas_call(
        functools.partial(near_forward_kernel, n, slots, hubs),
        out_shape=(
            pltpu.HBM((rows, width), F32),
            pltpu.HBM((PLAN,), I32),
            pltpu.HBM((rows, n * slots + LANES), BF16),
        ),
        in_specs=[HBM] * 5 + [VMEM, HBM],
        out_specs=(HBM, HBM, HBM),
        scratch_shapes=[
            pltpu.SMEM(tile_rows.shape, I32),
            pltpu.SMEM(tile_cols.shape, I32),
            pltpu.SMEM(send_rows.shape, I32),
            pltpu.SMEM(send_count.shape, I32),
            pltpu.SMEM(hub_rows.shape, I32),
            pltpu.VMEM((rows, width), BF16),
            pltpu.VMEM((rows, width), F32),
            pltpu.VMEM((rows, n * slots + LANES), BF16),
            pltpu.SMEM((PLAN,), I32),
            pltpu.SMEM((4 * KEYS,), I32),
            DMA((6,)),
        ],
        compiler_params=params(20 << 20),
        cost_estimate=cost(4 << 30, 8 << 20),
        name="near_forward",
    )(
        *in_hbm(tile_rows, tile_cols, send_rows, send_count, hub_rows),
        *in_vmem(tiles),
        *in_hbm(features),
    )


def unpack_slots(n, slots, chunks, packed, into, at):
    def pair(q, _):
        for c in range(0, chunks, 2):
            spot = slice(SUBS + c * slots, SUBS + (c + 2) * slots)
            first = packed[2 * q, spot, :].astype(F32)
            second = packed[2 * q + 1, spot, :].astype(F32)
            for half in range(2):
                part = slice(half * slots, (half + 1) * slots)
                both = jnp.concatenate([first[part], second[part]], axis=0).astype(BF16)
                where = pl.ds(pl.multiple_of(at + q * 2 * slots, 2 * slots), 2 * slots)
                into[where, (c + half) * LANES : (c + half + 1) * LANES] = both
        return 0

    lax.fori_loop(0, n // 2, pair, 0, unroll=4)


def place():
    device = lax.axis_index("dom")
    out = jnp.zeros((), I32)
    for at, bit in enumerate(HALVED):
        out = out | (((device >> bit) & 1) << (len(HALVED) - 1 - at))
    return out


def forward_kernel(
    n, slots, hubs, tile_rows_in, tile_cols_in, plan_in, tiles, received, near_in, weight_in, cot_in,
    output, grad_agg_out, keep, give,
    tile_rows, tile_cols, plan, table, total, near, weight, cot, agg, grad_pre, grad_agg, out, sems, near_sems, cot_sems, out_sems, ga_sems,
):
    size = tiles.shape[1]
    rows, width = near.shape
    chunks = width // LANES
    blocks = rows // size
    step = 256
    steps = rows // step
    index = [
        start(a, b, sems.at[i])
        for i, (a, b) in enumerate(((plan_in, plan), (tile_rows_in, tile_rows), (tile_cols_in, tile_cols)))
    ]
    weight_copy = start(weight_in, weight, sems.at[3])
    pieces = [pl.ds(b * step, step) for b in range(steps)]
    arrivals = [
        (start(near_in.at[at], near.at[at], near_sems.at[b]), start(cot_in.at[at], cot.at[at], cot_sems.at[b]))
        for b, at in enumerate(pieces)
    ]
    total[...] = jnp.zeros_like(total)

    def four(q, _):
        parts = [received[4 * q + u, 0:SUBS, :].astype(F32) for u in range(4)]
        for c in range(chunks):
            quad = jnp.concatenate([part[c * hubs : (c + 1) * hubs] for part in parts], axis=0)
            table[rows_at(q, SUBS), c * LANES : (c + 1) * LANES] = quad.astype(BF16)
        return 0

    lax.fori_loop(0, n // 4, four, 0, unroll=2)
    unpack_slots(n, slots, chunks, received, table, n * hubs)
    for copy in index:
        copy.wait()
    run_plan(FAR_FWD, plan, tiles, lambda t: jnp.maximum(tile_cols[t] - blocks, 0), table, total, False)
    weight_copy.wait()
    for pair in arrivals:
        for copy in pair:
            copy.wait()

    def first(at):
        here = (total[at, :] + near[at, :]).astype(BF16)
        agg[at, :] = here
        return jnp.dot(here, weight[...], preferred_element_type=F32)

    sent = []
    pre = first(pieces[0])
    for b, at in enumerate(pieces):
        following = first(pieces[b + 1]) if b + 1 < steps else None
        sig = 0.5 * jnp.tanh(0.5 * pre) + 0.5
        out[at, :] = (pre * sig).astype(BF16)
        gp = (cot[at, :].astype(F32) * sig * (1.0 + pre * (1.0 - sig))).astype(BF16)
        grad_pre[at, :] = gp
        grad_agg[at, :] = lax.dot_general(
            gp, weight[...], (((1,), (1,)), ((), ())), preferred_element_type=F32
        ).astype(BF16)
        sent.append(start(out.at[at], output.at[at], out_sems.at[b]))
        sent.append(start(grad_agg.at[at], grad_agg_out.at[at], ga_sems.at[b]))
        pre = following
    scale = float(rows * n) ** -0.5
    term = total.at[pl.ds(0, width)]
    for c in range(0, width, 256):
        term[c : c + 256, :] = (
            lax.dot_general(
                agg[:, c : c + 256], grad_pre[...], (((0,), (0,)), ((), ())), preferred_element_type=F32
            )
            * scale
        )
    half = 1 << (len(HALVED) - 1)
    unit = width // (2 * half)
    mine = place()
    for b in range(half):
        spot = slice(b * unit, (b + 1) * unit)
        keep[spot, :] = term[rows_at(mine ^ b, unit), :]
        give[spot, :] = term[rows_at(mine ^ (b + half), unit), :].astype(BF16)
    for copy in sent:
        copy.wait()


def forward(n, slots, hubs, tile_rows, tile_cols, plan, tiles, received, near, weight, cotangent):
    rows, width = near.shape
    steps = rows // 256
    return pl.pallas_call(
        functools.partial(forward_kernel, n, slots, hubs),
        out_shape=(
            pltpu.HBM((rows, width), BF16),
            pltpu.HBM((rows, width), BF16),
            pltpu.VMEM((width // 2, width), F32),
            pltpu.VMEM((width // 2, width), BF16),
        ),
        in_specs=[HBM, HBM, HBM, VMEM, VMEM, HBM, HBM, HBM],
        out_specs=(HBM, HBM, VMEM, VMEM),
        scratch_shapes=[
            pltpu.SMEM(tile_rows.shape, I32),
            pltpu.SMEM(tile_cols.shape, I32),
            pltpu.SMEM((PLAN,), I32),
            pltpu.VMEM((n * (slots + hubs), width), BF16),
            pltpu.VMEM((rows, width), F32),
            pltpu.VMEM((rows, width), F32),
            pltpu.VMEM((width, width), BF16),
            pltpu.VMEM((rows, width), BF16),
            pltpu.VMEM((rows, width), BF16),
            pltpu.VMEM((rows, width), BF16),
            pltpu.VMEM((rows, width), BF16),
            pltpu.VMEM((rows, width), BF16),
            DMA((4,)),
            DMA((steps,)),
            DMA((steps,)),
            DMA((steps,)),
            DMA((steps,)),
        ],
        compiler_params=params(28 << 20),
        cost_estimate=cost(8 << 30, 16 << 20),
        name="forward",
    )(*in_hbm(tile_rows, tile_cols, plan), *in_vmem(tiles, received), *in_hbm(near, weight, cotangent))


def far_backward_kernel(
    n, slots, hubs, tile_rows_in, plan_in, tiles, grad_agg_in, out, tile_rows, plan, grad_agg, total, staged, sems
):
    chunks = grad_agg.shape[1] // LANES
    moves = ((plan_in, plan), (tile_rows_in, tile_rows), (grad_agg_in, grad_agg))
    copies = [start(a, b, sems.at[i]) for i, (a, b) in enumerate(moves)]
    total[...] = jnp.zeros_like(total)
    for copy in copies:
        copy.wait()
    run_plan(FAR_BWD, plan, tiles, lambda t: tile_rows[t], grad_agg, total, True)

    def two(q, _):
        both = total[rows_at(q, 2 * hubs), :]
        for u in range(2):
            mine = both[u * hubs : (u + 1) * hubs]
            staged[2 * q + u, 0:SUBS, :] = jnp.concatenate(
                [mine[:, c * LANES : (c + 1) * LANES] for c in range(chunks)], axis=0
            ).astype(BF16)
            halo = total[pl.ds(pl.multiple_of(n * hubs + (2 * q + u) * slots, slots), slots), :]
            for c in range(0, chunks, 2):
                pair = jnp.concatenate(
                    [halo[:, c * LANES : (c + 1) * LANES], halo[:, (c + 1) * LANES : (c + 2) * LANES]], axis=0
                )
                staged[2 * q + u, SUBS + c * slots : SUBS + (c + 2) * slots, :] = pair.astype(BF16)
        return 0

    lax.fori_loop(0, n // 2, two, 0, unroll=2)
    start(staged, out, sems.at[0]).wait()


def far_backward(n, slots, hubs, tile_rows, plan, tiles, grad_agg):
    width = grad_agg.shape[1]
    packed = (n, (slots + hubs) * width // LANES, LANES)
    return pl.pallas_call(
        functools.partial(far_backward_kernel, n, slots, hubs),
        out_shape=pltpu.HBM(packed, BF16),
        in_specs=[HBM, HBM, VMEM, HBM],
        out_specs=HBM,
        scratch_shapes=[
            pltpu.SMEM(tile_rows.shape, I32),
            pltpu.SMEM((PLAN,), I32),
            pltpu.VMEM(grad_agg.shape, BF16),
            pltpu.VMEM((n * (slots + hubs), width), F32),
            pltpu.VMEM(packed, BF16),
            DMA((3,)),
        ],
        compiler_params=params(12 << 20),
        cost_estimate=cost(4 << 30, 8 << 20),
        name="far_backward",
    )(*in_hbm(tile_rows, plan), *in_vmem(tiles), *in_hbm(grad_agg))


def near_backward_kernel(
    tile_rows_in, plan_in, tiles_in, grad_agg_in, out, tile_rows, plan, tiles, grad_agg, total, sems
):
    near = tiles_in.at[pl.ds(0, LOC_TILES)]
    moves = ((tile_rows_in, tile_rows), (plan_in, plan), (grad_agg_in, grad_agg), (near, tiles))
    copies = [start(a, b, sems.at[i]) for i, (a, b) in enumerate(moves)]
    total[...] = jnp.zeros_like(total)
    for copy in copies:
        copy.wait()
    run_plan(NEAR_BWD, plan, tiles, lambda t: tile_rows[t], grad_agg, total, True)
    out[...] = total[...].astype(BF16)


def near_backward(tile_rows, plan, tiles, grad_agg):
    return pl.pallas_call(
        near_backward_kernel,
        out_shape=pltpu.VMEM(grad_agg.shape, BF16),
        in_specs=[HBM] * 4,
        out_specs=VMEM,
        scratch_shapes=[
            pltpu.SMEM(tile_rows.shape, I32),
            pltpu.SMEM((PLAN,), I32),
            pltpu.VMEM((LOC_TILES,) + tiles.shape[1:], BF16),
            pltpu.VMEM(grad_agg.shape, BF16),
            pltpu.VMEM(grad_agg.shape, F32),
            DMA((4,)),
        ],
        compiler_params=params(16 << 20),
        cost_estimate=cost(0, 0),
        name="near_backward",
    )(*in_hbm(tile_rows, plan, tiles, grad_agg))


def collect_kernel(
    n, slots, hubs, near, spread_in, returned, out, spread, table, staged, spread_sems, out_sems
):
    rows, width = staged.shape
    chunks = width // LANES
    step = 256
    pieces = [pl.ds(at, step) for at in range(0, rows, step)]
    arrival = start(spread_in, spread, spread_sems.at[0])
    unpack_slots(n, slots, chunks, returned, table, 0)
    hub = lax.fori_loop(
        0, n, lambda s, held: held + returned[s, 0:SUBS, :].astype(F32), jnp.zeros((SUBS, LANES), F32), unroll=8
    )
    group = lax.broadcasted_iota(I32, (SUBS, LANES), 0) // hubs
    base = n * slots
    table[base : base + LANES, :] = jnp.zeros((LANES, width), BF16)
    upper = hub.astype(BF16).astype(F32)
    for at, part in ((0, upper), (SUBS, hub - upper)):
        for c in range(chunks):
            table[base + at : base + at + SUBS, c * LANES : (c + 1) * LANES] = jnp.where(
                group == c, part, 0.0
            ).astype(BF16)
    sent = []
    arrival.wait()
    for b, at in enumerate(pieces):
        more = jnp.dot(spread[at, :], table[...], preferred_element_type=F32)
        staged[at, :] = (near[at, :].astype(F32) + more).astype(BF16)
        sent.append(start(staged.at[at], out.at[at], out_sems.at[b]))
    for copy in sent:
        copy.wait()


def collect(n, slots, hubs, near, spread, returned):
    rows, width = near.shape
    table = n * slots + LANES
    return pl.pallas_call(
        functools.partial(collect_kernel, n, slots, hubs),
        out_shape=pltpu.HBM((rows, width), BF16),
        in_specs=[VMEM, HBM, VMEM],
        out_specs=HBM,
        scratch_shapes=[
            pltpu.VMEM((rows, table), BF16),
            pltpu.VMEM((table, width), BF16),
            pltpu.VMEM((rows, width), BF16),
            DMA((1,)),
            DMA((rows // 256,)),
        ],
        compiler_params=params(16 << 20),
        cost_estimate=cost(32 << 30, 8 << 20),
        name="collect",
    )(*in_vmem(near), *in_hbm(spread), *in_vmem(returned))


def order_kernel(first, second, out):
    half = 1 << (len(HALVED) - 1)
    unit = out.shape[0] // (2 * half)
    mine = place()
    for b in range(half):
        spot = slice(b * unit, (b + 1) * unit)
        out[rows_at(mine ^ b, unit), :] = first[spot, :].astype(F32)
        out[rows_at(mine ^ (b + half), unit), :] = second[spot, :].astype(F32)


def exchange(x, n, mask):
    return lax.ppermute(x, "dom", [(i, i ^ mask) for i in range(n)])


def tie(*arrays):
    return lax.optimization_barrier(arrays)


def all_to_all(x):
    return lax.all_to_all(x, "dom", split_axis=0, concat_axis=0, tiled=True)


def per_device(
    features, weight, cotangent, tile_values, tile_rows, tile_cols, hub_rows, send_rows, send_count
):
    n = lax.axis_size("dom")
    slots, hubs = send_rows.shape[2], hub_rows.shape[0]
    send_rows = jnp.swapaxes(send_rows, 1, 2)

    packed = pack_rows(n, send_rows, send_count, hub_rows, features)
    received = all_to_all(packed)
    near, plan, spread = near_forward(
        n, tile_rows, tile_cols, send_rows, send_count, hub_rows, tile_values, features
    )
    output, grad_agg, keep, give = forward(
        n, slots, hubs, tile_rows, tile_cols, plan, tile_values, received, near, weight, cotangent
    )
    width = keep.shape[1]
    keep = keep + exchange(give, n, 1 << HALVED[0]).astype(F32)
    half = keep.shape[0] // 2
    keep, give, grad_agg = tie(keep[:half].astype(BF16), keep[half:].astype(BF16), grad_agg)
    got = exchange(give, n, 1 << HALVED[1])
    far = far_backward(n, slots, hubs, tile_rows, plan, tile_values, grad_agg)
    half = half // 2
    give = (keep[half:].astype(F32) + got[half:].astype(F32)).astype(BF16)
    keep = (keep[:half].astype(F32) + got[:half].astype(F32)).astype(BF16)
    keep, give, far = tie(keep, give, far)
    got = exchange(give, n, 1 << HALVED[2])
    returned = all_to_all(far)
    held, grad_agg = tie((keep.astype(F32) + got.astype(F32)).astype(BF16), grad_agg)
    for bit in range(n.bit_length() - 1):
        if bit not in HALVED:
            got = exchange(held, n, 1 << bit)
            held = (held.astype(F32) + got.astype(F32)).astype(BF16)
            if bit == 1:
                near_grad = near_backward(tile_rows, plan, tile_values, grad_agg)
                held, near_grad = tie(held, near_grad)
            else:
                held = lax.optimization_barrier(held)
    held, near_grad, returned = tie(held, near_grad, returned)
    one, other = 1 << HALVED[1], 1 << HALVED[2]
    parts = [exchange(held, n, mask) for mask in (other, one, one | other)]
    grad_features = collect(n, slots, hubs, near_grad, spread, returned)
    held, grad_features = tie(jnp.concatenate([held] + parts, axis=0), grad_features)
    grad_weight = pl.pallas_call(
        order_kernel,
        out_shape=jax.ShapeDtypeStruct((width, width), F32),
        in_specs=[VMEM, VMEM],
        out_specs=VMEM,
        compiler_params=params(4 << 20),
        name="order",
    )(held, exchange(held, n, 1 << HALVED[0]))
    return (output, grad_features, grad_weight)


def solution(mesh):
    placed = (
        P("dom", None),
        P(),
        P("dom", None),
        P("dom", None, None),
        P("dom"),
        P("dom"),
        P("dom"),
        P("dom", None, None),
        P("dom", None),
    )
    return jax.shard_map(
        per_device,
        mesh=mesh,
        in_specs=placed,
        out_specs=(P("dom", None), P("dom", None), P()),
        check_vma=False,
    )
```

```python
import functools

import jax
import jax.numpy as jnp
from jax import lax
from jax.experimental import pallas as pl
from jax.experimental.pallas import tpu as pltpu
from jax.sharding import PartitionSpec as P

LOC_TILES = 64
LANES = 128
SUBS = 16
NONE = 255
KEYS = 32
LIST = 64
UNROLL = 8
HALVED = (0, 2, 1)
NEAR_FWD, FAR_FWD, NEAR_BWD, FAR_BWD = range(4)
COUNTS = 4 * LIST
PLAN = COUNTS + LANES
VMEM = pl.BlockSpec(memory_space=pltpu.VMEM)
HBM = pl.BlockSpec(memory_space=pltpu.HBM)
DMA = pltpu.SemaphoreType.DMA
BF16, F32, I32 = jnp.bfloat16, jnp.float32, jnp.int32


def rows_at(block, size):
    return pl.ds(pl.multiple_of(block * size, size), size)


def params(limit):
    return pltpu.CompilerParams(vmem_limit_bytes=limit)


def in_hbm(*arrays):
    return [pltpu.with_memory_space_constraint(a, pltpu.HBM) for a in arrays]


def in_vmem(*arrays):
    return [pltpu.with_memory_space_constraint(a, pltpu.VMEM) for a in arrays]


def cost(flops, moved):
    return pl.CostEstimate(flops=flops, bytes_accessed=moved, transcendentals=0)


def start(source, target, sem):
    copy = pltpu.make_async_copy(source, target, sem)
    copy.start()
    return copy


def pack_kernel(
    n, slots, hubs, send_rows_in, send_count_in, hub_rows_in, feats_in, out,
    send_rows, send_count, hub_rows, feats, select, found, staged, sems, feat_sems, out_sems,
):
    rows, width = feats.shape
    chunks = width // LANES
    copies = [
        start(a, b, sems.at[i])
        for i, (a, b) in enumerate(
            (
                (send_rows_in, send_rows),
                (send_count_in, send_count),
                (hub_rows_in, hub_rows),
            )
        )
    ]
    pieces = [slice(at, at + rows // 2) for at in range(0, rows, rows // 2)]
    arrivals = [start(feats_in.at[at], feats.at[at], feat_sems.at[k]) for k, at in enumerate(pieces)]
    sub = lax.broadcasted_iota(I32, (2 * slots, LANES), 0)
    lane = lax.broadcasted_iota(I32, (2 * slots, LANES), 1)
    for copy in copies:
        copy.wait()

    def put(at, column):
        for part in range(rows // LANES):
            hit = jnp.where(column == lane + part * LANES, 1.0, 0.0)
            select[rows_at(at, 2 * slots), part * LANES : (part + 1) * LANES] = hit.astype(BF16)

    column = jnp.zeros((2 * slots, LANES), I32)
    for row in range(hubs * chunks):
        column = jnp.where(sub == row, hub_rows[row % hubs], column)
    put(0, column)

    def pair(q, _):
        column = jnp.full((2 * slots, LANES), -1, I32)
        for half in range(2):
            dest = 2 * q + half
            count = send_count[0, dest]
            for k in range(slots):
                row = jnp.where(k < count, send_rows[0, k, dest], -1)
                column = jnp.where(sub == half * slots + k, row, column)
        put(q + 1, column)
        return 0

    lax.fori_loop(0, n // 2, pair, 0, unroll=2)
    group = sub // hubs
    for k, at in enumerate(pieces):
        arrivals[k].wait()
        part = jnp.dot(select[:, at], feats[at, :], preferred_element_type=F32)
        found[...] = part if k == 0 else found[...] + part
    hub = jnp.zeros((hubs * chunks, LANES), F32)
    for c in range(chunks):
        hub = jnp.where(group == c, found[0 : 2 * slots, c * LANES : (c + 1) * LANES], hub)
    hub = hub.astype(BF16)
    per = LANES // slots
    sent = []
    for b in range(n // per):
        for s in range(per):
            dest = b * per + s
            staged[dest, 0:SUBS, :] = hub
            mine = found[2 * slots + dest * slots : 2 * slots + (dest + 1) * slots, :]
            for c in range(0, chunks, 2):
                both = jnp.concatenate(
                    [mine[:, c * LANES : (c + 1) * LANES], mine[:, (c + 1) * LANES : (c + 2) * LANES]], axis=0
                )
                staged[dest, SUBS + c * slots : SUBS + (c + 2) * slots, :] = both.astype(BF16)
        group_of = pl.ds(b * per, per)
        sent.append(start(staged.at[group_of], out.at[group_of], out_sems.at[b]))
    for copy in sent:
        copy.wait()


def pack_rows(n, send_rows, send_count, hub_rows, features):
    slots, hubs = send_rows.shape[1], hub_rows.shape[0]
    rows, width = features.shape
    packed = (n, (slots + hubs) * width // LANES, LANES)
    return pl.pallas_call(
        functools.partial(pack_kernel, n, slots, hubs),
        out_shape=pltpu.HBM(packed, BF16),
        in_specs=[HBM] * 4,
        out_specs=HBM,
        scratch_shapes=[
            pltpu.SMEM(send_rows.shape, I32),
            pltpu.SMEM(send_count.shape, I32),
            pltpu.SMEM(hub_rows.shape, I32),
            pltpu.VMEM((rows, width), BF16),
            pltpu.VMEM((n * slots + 2 * slots, rows), BF16),
            pltpu.VMEM((n * slots + 2 * slots, width), F32),
            pltpu.VMEM(packed, BF16),
            DMA((3,)),
            DMA((2,)),
            DMA((n * slots // LANES,)),
        ],
        compiler_params=params(16 << 20),
        name="pack_rows",
    )(*in_hbm(send_rows, send_count, hub_rows, features))


def make_plan(tile_rows, tile_cols, blocks, plan, waiting):
    def clear(i, _):
        waiting[i] = NONE
        return 0

    lax.fori_loop(0, 4 * KEYS, clear, 0, unroll=8)
    for kind in range(4):
        plan[COUNTS + kind] = 0

    def add(kind, key, t):
        slot = kind * KEYS + key
        first, count = waiting[slot], plan[COUNTS + kind]
        pair = first != NONE
        plan[kind * LIST + count] = (key << 16) | (first << 8) | t
        plan[COUNTS + kind] = count + pair.astype(I32)
        waiting[slot] = jnp.where(pair, NONE, t)

    def tile(t, _):
        row, col = tile_rows[t], tile_cols[t]
        far = (col >= blocks).astype(I32)
        add(NEAR_FWD + far, row, t)
        add(NEAR_BWD + far, col - blocks * far, t)
        return 0

    lax.fori_loop(0, tile_rows.shape[0], tile, 0)
    for kind in range(4):

        def left(key, count, kind=kind):
            first = waiting[kind * KEYS + key]
            plan[kind * LIST + count] = (key << 16) | (first << 8) | NONE
            return count + (first != NONE).astype(I32)

        count = lax.fori_loop(0, KEYS, left, plan[COUNTS + kind])
        plan[COUNTS + kind] = count
        for u in range(UNROLL):
            plan[kind * LIST + count + u] = (NONE << 8) | NONE


def run_plan(kind, plan, tiles, source_of, source, total, transposed):
    size, last = tiles.shape[1], tiles.shape[0] - 1
    axis = 0 if transposed else 1

    def group(g, _):
        for u in range(UNROLL):
            word = plan[kind * LIST + g * UNROLL + u]
            key, picks = word >> 16, ((word >> 8) & 255, word & 255)
            left, right = [], []
            for pick in picks:
                t = jnp.minimum(pick, last)
                left.append(jnp.where(pick == NONE, jnp.zeros((size, size), BF16), tiles[t]))
                right.append(source[rows_at(source_of(t), size), :])
            total[rows_at(key, size), :] += lax.dot_general(
                jnp.concatenate(left, axis=axis),
                jnp.concatenate(right, axis=0),
                (((axis,), (0,)), ((), ())),
                preferred_element_type=F32,
            )
        return 0

    lax.fori_loop(0, (plan[COUNTS + kind] + UNROLL - 1) // UNROLL, group, 0)


def make_spread(n, slots, hubs, chunks, send_rows, send_count, hub_rows, spread):
    rows = spread.shape[0]
    lane = lax.broadcasted_iota(I32, (SUBS, LANES), 1)
    sub = lax.broadcasted_iota(I32, (SUBS, LANES), 0)

    def put(part, targets):
        def rows_of(b, _):
            hit = jnp.where(targets == sub + b * SUBS, 1.0, 0.0)
            spread[rows_at(b, SUBS), part * LANES : (part + 1) * LANES] = hit.astype(BF16)
            return 0

        lax.fori_loop(0, rows // SUBS, rows_of, 0, unroll=8)

    per = LANES // slots
    for part in range(n * slots // LANES):

        def dest(s, targets, part=part):
            count = send_count[0, part * per + s]
            for k in range(slots):
                row = jnp.where(k < count, send_rows[0, k, part * per + s], -1)
                targets = jnp.where(lane == s * slots + k, row, targets)
            return targets

        put(part, lax.fori_loop(0, per, dest, jnp.full((SUBS, LANES), -1, I32)))
    targets = jnp.full((SUBS, LANES), -1, I32)
    for at in range(2 * hubs * chunks):
        targets = jnp.where(lane == at, hub_rows[at % hubs], targets)
    put(n * slots // LANES, targets)


def near_forward_kernel(
    n, slots, hubs, tile_rows_in, tile_cols_in, send_rows_in, send_count_in, hub_rows_in, tiles, feats_in,
    near_out, plan_out, spread_out,
    tile_rows, tile_cols, send_rows, send_count, hub_rows, feats, total, spread, plan, waiting, sems,
):
    rows, width = feats.shape
    blocks = rows // tiles.shape[1]
    moves = (
        (tile_rows_in, tile_rows),
        (tile_cols_in, tile_cols),
        (send_rows_in, send_rows),
        (send_count_in, send_count),
        (hub_rows_in, hub_rows),
        (feats_in, feats),
    )
    copies = [start(a, b, sems.at[i]) for i, (a, b) in enumerate(moves)]
    total[...] = jnp.zeros_like(total)
    copies[0].wait()
    copies[1].wait()
    make_plan(tile_rows, tile_cols, blocks, plan, waiting)
    sent = [start(plan, plan_out, sems.at[0])]
    for copy in copies[2:]:
        copy.wait()
    run_plan(NEAR_FWD, plan, tiles, lambda t: jnp.minimum(tile_cols[t], blocks - 1), feats, total, False)
    sent.append(start(total, near_out, sems.at[1]))
    make_spread(n, slots, hubs, width // LANES, send_rows, send_count, hub_rows, spread)
    sent.append(start(spread, spread_out, sems.at[2]))
    for copy in sent:
        copy.wait()


def near_forward(n, tile_rows, tile_cols, send_rows, send_count, hub_rows, tiles, features):
    rows, width = features.shape
    slots, hubs = send_rows.shape[1], hub_rows.shape[0]
    return pl.pallas_call(
        functools.partial(near_forward_kernel, n, slots, hubs),
        out_shape=(
            pltpu.HBM((rows, width), F32),
            pltpu.HBM((PLAN,), I32),
            pltpu.HBM((rows, n * slots + LANES), BF16),
        ),
        in_specs=[HBM] * 5 + [VMEM, HBM],
        out_specs=(HBM, HBM, HBM),
        scratch_shapes=[
            pltpu.SMEM(tile_rows.shape, I32),
            pltpu.SMEM(tile_cols.shape, I32),
            pltpu.SMEM(send_rows.shape, I32),
            pltpu.SMEM(send_count.shape, I32),
            pltpu.SMEM(hub_rows.shape, I32),
            pltpu.VMEM((rows, width), BF16),
            pltpu.VMEM((rows, width), F32),
            pltpu.VMEM((rows, n * slots + LANES), BF16),
            pltpu.SMEM((PLAN,), I32),
            pltpu.SMEM((4 * KEYS,), I32),
            DMA((6,)),
        ],
        compiler_params=params(20 << 20),
        cost_estimate=cost(4 << 30, 8 << 20),
        name="near_forward",
    )(
        *in_hbm(tile_rows, tile_cols, send_rows, send_count, hub_rows),
        *in_vmem(tiles),
        *in_hbm(features),
    )


def unpack_slots(n, slots, chunks, packed, into, at):
    def pair(q, _):
        for c in range(0, chunks, 2):
            spot = slice(SUBS + c * slots, SUBS + (c + 2) * slots)
            first = packed[2 * q, spot, :].astype(F32)
            second = packed[2 * q + 1, spot, :].astype(F32)
            for half in range(2):
                part = slice(half * slots, (half + 1) * slots)
                both = jnp.concatenate([first[part], second[part]], axis=0).astype(BF16)
                where = pl.ds(pl.multiple_of(at + q * 2 * slots, 2 * slots), 2 * slots)
                into[where, (c + half) * LANES : (c + half + 1) * LANES] = both
        return 0

    lax.fori_loop(0, n // 2, pair, 0, unroll=4)


def pack_grads(n, slots, hubs, chunks, total, staged):
    def two(q, _):
        both = total[rows_at(q, 2 * hubs), :]
        for u in range(2):
            mine = both[u * hubs : (u + 1) * hubs]
            staged[2 * q + u, 0:SUBS, :] = jnp.concatenate(
                [mine[:, c * LANES : (c + 1) * LANES] for c in range(chunks)], axis=0
            ).astype(BF16)
            halo = total[pl.ds(pl.multiple_of(n * hubs + (2 * q + u) * slots, slots), slots), :]
            for c in range(0, chunks, 2):
                pair = jnp.concatenate(
                    [halo[:, c * LANES : (c + 1) * LANES], halo[:, (c + 1) * LANES : (c + 2) * LANES]], axis=0
                )
                staged[2 * q + u, SUBS + c * slots : SUBS + (c + 2) * slots, :] = pair.astype(BF16)
        return 0

    lax.fori_loop(0, n // 2, two, 0, unroll=2)


def place():
    device = lax.axis_index("dom")
    out = jnp.zeros((), I32)
    for at, bit in enumerate(HALVED):
        out = out | (((device >> bit) & 1) << (len(HALVED) - 1 - at))
    return out


def forward_kernel(
    n, slots, hubs, tile_rows_in, tile_cols_in, plan_in, tiles, received, near_in, weight_in, cot_in,
    output, grad_agg_out, far_out, keep, give,
    tile_rows, tile_cols, plan, table, total, far_total, staged, near, weight, cot, agg, grad_pre, grad_agg, out, sems, near_sems, cot_sems, out_sems, ga_sems,
):
    size = tiles.shape[1]
    rows, width = near.shape
    chunks = width // LANES
    blocks = rows // size
    step = 256
    steps = rows // step
    index = [
        start(a, b, sems.at[i])
        for i, (a, b) in enumerate(((plan_in, plan), (tile_rows_in, tile_rows), (tile_cols_in, tile_cols)))
    ]
    weight_copy = start(weight_in, weight, sems.at[3])
    pieces = [pl.ds(b * step, step) for b in range(steps)]
    arrivals = [
        (start(near_in.at[at], near.at[at], near_sems.at[b]), start(cot_in.at[at], cot.at[at], cot_sems.at[b]))
        for b, at in enumerate(pieces)
    ]
    total[...] = jnp.zeros_like(total)
    far_total[...] = jnp.zeros_like(far_total)

    def four(q, _):
        parts = [received[4 * q + u, 0:SUBS, :].astype(F32) for u in range(4)]
        for c in range(chunks):
            quad = jnp.concatenate([part[c * hubs : (c + 1) * hubs] for part in parts], axis=0)
            table[rows_at(q, SUBS), c * LANES : (c + 1) * LANES] = quad.astype(BF16)
        return 0

    lax.fori_loop(0, n // 4, four, 0, unroll=2)
    unpack_slots(n, slots, chunks, received, table, n * hubs)
    for copy in index:
        copy.wait()
    run_plan(FAR_FWD, plan, tiles, lambda t: jnp.maximum(tile_cols[t] - blocks, 0), table, total, False)
    weight_copy.wait()

    def arrive(blocks_of):
        for pair in arrivals[blocks_of]:
            for copy in pair:
                copy.wait()

    def first(at):
        here = (total[at, :] + near[at, :]).astype(BF16)
        agg[at, :] = here
        return jnp.dot(here, weight[...], preferred_element_type=F32)

    sent = []
    arrive(slice(0, steps // 2))
    pre = first(pieces[0])
    for b, at in enumerate(pieces):
        if b + 1 == steps // 2:
            arrive(slice(steps // 2, steps))
        following = first(pieces[b + 1]) if b + 1 < steps else None
        sig = 0.5 * jnp.tanh(0.5 * pre) + 0.5
        out[at, :] = (pre * sig).astype(BF16)
        gp = (cot[at, :].astype(F32) * sig * (1.0 + pre * (1.0 - sig))).astype(BF16)
        grad_pre[at, :] = gp
        grad_agg[at, :] = lax.dot_general(
            gp, weight[...], (((1,), (1,)), ((), ())), preferred_element_type=F32
        ).astype(BF16)
        sent.append(start(out.at[at], output.at[at], out_sems.at[b]))
        sent.append(start(grad_agg.at[at], grad_agg_out.at[at], ga_sems.at[b]))
        pre = following
    run_plan(FAR_BWD, plan, tiles, lambda t: tile_rows[t], grad_agg, far_total, True)
    pack_grads(n, slots, hubs, chunks, far_total, staged)
    sent.append(start(staged, far_out, sems.at[0]))
    scale = float(rows * n) ** -0.5
    term = total.at[pl.ds(0, width)]
    for c in range(0, width, 256):
        term[c : c + 256, :] = (
            lax.dot_general(
                agg[:, c : c + 256], grad_pre[...], (((0,), (0,)), ((), ())), preferred_element_type=F32
            )
            * scale
        )
    half = 1 << (len(HALVED) - 1)
    unit = width // (2 * half)
    mine = place()
    for b in range(half):
        spot = slice(b * unit, (b + 1) * unit)
        keep[spot, :] = term[rows_at(mine ^ b, unit), :]
        give[spot, :] = term[rows_at(mine ^ (b + half), unit), :].astype(BF16)
    for copy in sent:
        copy.wait()


def forward(n, slots, hubs, tile_rows, tile_cols, plan, tiles, received, near, weight, cotangent):
    rows, width = near.shape
    packed = (n, (slots + hubs) * width // LANES, LANES)
    steps = rows // 256
    return pl.pallas_call(
        functools.partial(forward_kernel, n, slots, hubs),
        out_shape=(
            pltpu.HBM((rows, width), BF16),
            pltpu.HBM((rows, width), BF16),
            pltpu.HBM(packed, BF16),
            pltpu.VMEM((width // 2, width), F32),
            pltpu.VMEM((width // 2, width), BF16),
        ),
        in_specs=[HBM, HBM, HBM, VMEM, VMEM, HBM, HBM, HBM],
        out_specs=(HBM, HBM, HBM, VMEM, VMEM),
        scratch_shapes=[
            pltpu.SMEM(tile_rows.shape, I32),
            pltpu.SMEM(tile_cols.shape, I32),
            pltpu.SMEM((PLAN,), I32),
            pltpu.VMEM((n * (slots + hubs), width), BF16),
            pltpu.VMEM((rows, width), F32),
            pltpu.VMEM((n * (slots + hubs), width), F32),
            pltpu.VMEM(packed, BF16),
            pltpu.VMEM((rows, width), F32),
            pltpu.VMEM((width, width), BF16),
            pltpu.VMEM((rows, width), BF16),
            pltpu.VMEM((rows, width), BF16),
            pltpu.VMEM((rows, width), BF16),
            pltpu.VMEM((rows, width), BF16),
            pltpu.VMEM((rows, width), BF16),
            DMA((4,)),
            DMA((steps,)),
            DMA((steps,)),
            DMA((steps,)),
            DMA((steps,)),
        ],
        compiler_params=params(28 << 20),
        cost_estimate=cost(8 << 30, 16 << 20),
        name="forward",
    )(*in_hbm(tile_rows, tile_cols, plan), *in_vmem(tiles, received), *in_hbm(near, weight, cotangent))


def near_backward_kernel(
    tile_rows_in, plan_in, tiles_in, grad_agg_in, out, tile_rows, plan, tiles, grad_agg, total, sems
):
    near = tiles_in.at[pl.ds(0, LOC_TILES)]
    moves = ((tile_rows_in, tile_rows), (plan_in, plan), (grad_agg_in, grad_agg), (near, tiles))
    copies = [start(a, b, sems.at[i]) for i, (a, b) in enumerate(moves)]
    total[...] = jnp.zeros_like(total)
    for copy in copies:
        copy.wait()
    run_plan(NEAR_BWD, plan, tiles, lambda t: tile_rows[t], grad_agg, total, True)
    out[...] = total[...].astype(BF16)


def near_backward(tile_rows, plan, tiles, grad_agg):
    return pl.pallas_call(
        near_backward_kernel,
        out_shape=pltpu.VMEM(grad_agg.shape, BF16),
        in_specs=[HBM] * 4,
        out_specs=VMEM,
        scratch_shapes=[
            pltpu.SMEM(tile_rows.shape, I32),
            pltpu.SMEM((PLAN,), I32),
            pltpu.VMEM((LOC_TILES,) + tiles.shape[1:], BF16),
            pltpu.VMEM(grad_agg.shape, BF16),
            pltpu.VMEM(grad_agg.shape, F32),
            DMA((4,)),
        ],
        compiler_params=params(16 << 20),
        cost_estimate=cost(0, 0),
        name="near_backward",
    )(*in_hbm(tile_rows, plan, tiles, grad_agg))


def collect_kernel(
    n, slots, hubs, near, spread_in, returned, out, spread, table, staged, spread_sems, out_sems
):
    rows, width = staged.shape
    chunks = width // LANES
    step = 256
    pieces = [pl.ds(at, step) for at in range(0, rows, step)]
    arrival = start(spread_in, spread, spread_sems.at[0])
    unpack_slots(n, slots, chunks, returned, table, 0)
    hub = lax.fori_loop(
        0, n, lambda s, held: held + returned[s, 0:SUBS, :].astype(F32), jnp.zeros((SUBS, LANES), F32), unroll=8
    )
    group = lax.broadcasted_iota(I32, (SUBS, LANES), 0) // hubs
    base = n * slots
    table[base : base + LANES, :] = jnp.zeros((LANES, width), BF16)
    upper = hub.astype(BF16).astype(F32)
    for at, part in ((0, upper), (SUBS, hub - upper)):
        for c in range(chunks):
            table[base + at : base + at + SUBS, c * LANES : (c + 1) * LANES] = jnp.where(
                group == c, part, 0.0
            ).astype(BF16)
    sent = []
    arrival.wait()
    for b, at in enumerate(pieces):
        more = jnp.dot(spread[at, :], table[...], preferred_element_type=F32)
        staged[at, :] = (near[at, :].astype(F32) + more).astype(BF16)
        sent.append(start(staged.at[at], out.at[at], out_sems.at[b]))
    for copy in sent:
        copy.wait()


def collect(n, slots, hubs, near, spread, returned):
    rows, width = near.shape
    table = n * slots + LANES
    return pl.pallas_call(
        functools.partial(collect_kernel, n, slots, hubs),
        out_shape=pltpu.HBM((rows, width), BF16),
        in_specs=[VMEM, HBM, VMEM],
        out_specs=HBM,
        scratch_shapes=[
            pltpu.VMEM((rows, table), BF16),
            pltpu.VMEM((table, width), BF16),
            pltpu.VMEM((rows, width), BF16),
            DMA((1,)),
            DMA((rows // 256,)),
        ],
        compiler_params=params(16 << 20),
        cost_estimate=cost(32 << 30, 8 << 20),
        name="collect",
    )(*in_vmem(near), *in_hbm(spread), *in_vmem(returned))


def order_kernel(first, second, out):
    half = 1 << (len(HALVED) - 1)
    unit = out.shape[0] // (2 * half)
    mine = place()
    for b in range(half):
        spot = slice(b * unit, (b + 1) * unit)
        out[rows_at(mine ^ b, unit), :] = first[spot, :].astype(F32)
        out[rows_at(mine ^ (b + half), unit), :] = second[spot, :].astype(F32)


def exchange(x, n, mask):
    return lax.ppermute(x, "dom", [(i, i ^ mask) for i in range(n)])


def tie(*arrays):
    return lax.optimization_barrier(arrays)


def all_to_all(x):
    return lax.all_to_all(x, "dom", split_axis=0, concat_axis=0, tiled=True)


def per_device(
    features, weight, cotangent, tile_values, tile_rows, tile_cols, hub_rows, send_rows, send_count
):
    n = lax.axis_size("dom")
    slots, hubs = send_rows.shape[2], hub_rows.shape[0]
    width = features.shape[1]
    send_rows = jnp.swapaxes(send_rows, 1, 2)

    packed = pack_rows(n, send_rows, send_count, hub_rows, features)
    received = all_to_all(packed)
    near, plan, spread = near_forward(
        n, tile_rows, tile_cols, send_rows, send_count, hub_rows, tile_values, features
    )
    output, grad_agg, far, keep, give = forward(
        n, slots, hubs, tile_rows, tile_cols, plan, tile_values, received, near, weight, cotangent
    )
    core, one, other = (1 << bit for bit in HALVED)
    got = exchange(give, n, core)
    quarters = (keep + got.astype(F32)).astype(BF16).reshape(4, keep.shape[0] // 4, width)
    *quarters, far, grad_agg = tie(*(quarters[i] for i in range(4)), far, grad_agg)
    parts = [quarters[0]] + [exchange(quarters[i], n, mask) for i, mask in ((1, other), (2, one), (3, one | other))]
    returned = all_to_all(far)
    a, b, c, d = (part.astype(F32) for part in parts)
    near_grad = near_backward(tile_rows, plan, tile_values, grad_agg)
    held, near_grad = tie(((a + b) + (c + d)).astype(BF16), near_grad)
    parts = [held] + [exchange(held, n, mask) for mask in (8, 16, 24)]
    a, b, c, d = (part.astype(F32) for part in parts)
    held = lax.optimization_barrier(((a + b) + (c + d)).astype(BF16))
    for bit in range(5, n.bit_length() - 1):
        held = (held.astype(F32) + exchange(held, n, 1 << bit).astype(F32)).astype(BF16)
    held, near_grad, returned = tie(held, near_grad, returned)
    parts = [exchange(held, n, mask) for mask in (other, one, one | other)]
    grad_features = collect(n, slots, hubs, near_grad, spread, returned)
    held, grad_features = tie(jnp.concatenate([held] + parts, axis=0), grad_features)
    grad_weight = pl.pallas_call(
        order_kernel,
        out_shape=jax.ShapeDtypeStruct((width, width), F32),
        in_specs=[VMEM, VMEM],
        out_specs=VMEM,
        compiler_params=params(4 << 20),
        name="order",
    )(held, exchange(held, n, core))
    return (output, grad_features, grad_weight)


def solution(mesh):
    placed = (
        P("dom", None),
        P(),
        P("dom", None),
        P("dom", None, None),
        P("dom"),
        P("dom"),
        P("dom"),
        P("dom", None, None),
        P("dom", None),
    )
    return jax.shard_map(
        per_device,
        mesh=mesh,
        in_specs=placed,
        out_specs=(P("dom", None), P("dom", None), P()),
        check_vma=False,
    )
```

```python
import functools

import jax
import jax.numpy as jnp
from jax import lax
from jax.experimental import pallas as pl
from jax.experimental.pallas import tpu as pltpu
from jax.sharding import PartitionSpec as P

LOC_TILES = 64
LANES = 128
SUBS = 16
NONE = 255
KEYS = 32
LIST = 64
UNROLL = 8
HALVED = (0, 2, 1)
NEAR_FWD, FAR_FWD, NEAR_BWD, FAR_BWD = range(4)
COUNTS = 4 * LIST
PLAN = COUNTS + LANES
VMEM = pl.BlockSpec(memory_space=pltpu.VMEM)
HBM = pl.BlockSpec(memory_space=pltpu.HBM)
DMA = pltpu.SemaphoreType.DMA
BF16, F32, I32 = jnp.bfloat16, jnp.float32, jnp.int32


def rows_at(block, size):
    return pl.ds(pl.multiple_of(block * size, size), size)


def params(limit):
    return pltpu.CompilerParams(vmem_limit_bytes=limit)


def in_hbm(*arrays):
    return [pltpu.with_memory_space_constraint(a, pltpu.HBM) for a in arrays]


def in_vmem(*arrays):
    return [pltpu.with_memory_space_constraint(a, pltpu.VMEM) for a in arrays]


def cost(flops, moved):
    return pl.CostEstimate(flops=flops, bytes_accessed=moved, transcendentals=0)


def start(source, target, sem):
    copy = pltpu.make_async_copy(source, target, sem)
    copy.start()
    return copy


def pack_kernel(
    n, slots, hubs, send_rows_in, send_count_in, hub_rows_in, feats_in, out,
    send_rows, send_count, hub_rows, feats, select, found, staged, sems, feat_sems, out_sems,
):
    rows, width = feats.shape
    chunks = width // LANES
    copies = [
        start(a, b, sems.at[i])
        for i, (a, b) in enumerate(
            (
                (send_rows_in, send_rows),
                (send_count_in, send_count),
                (hub_rows_in, hub_rows),
            )
        )
    ]
    pieces = [slice(at, at + rows // 2) for at in range(0, rows, rows // 2)]
    arrivals = [start(feats_in.at[at], feats.at[at], feat_sems.at[k]) for k, at in enumerate(pieces)]
    sub = lax.broadcasted_iota(I32, (2 * slots, LANES), 0)
    lane = lax.broadcasted_iota(I32, (2 * slots, LANES), 1)
    for copy in copies:
        copy.wait()

    def put(at, column):
        for part in range(rows // LANES):
            hit = jnp.where(column == lane + part * LANES, 1.0, 0.0)
            select[rows_at(at, 2 * slots), part * LANES : (part + 1) * LANES] = hit.astype(BF16)

    column = jnp.zeros((2 * slots, LANES), I32)
    for row in range(hubs * chunks):
        column = jnp.where(sub == row, hub_rows[row % hubs], column)
    put(0, column)

    def pair(q, _):
        column = jnp.full((2 * slots, LANES), -1, I32)
        for half in range(2):
            dest = 2 * q + half
            count = send_count[0, dest]
            for k in range(slots):
                row = jnp.where(k < count, send_rows[0, k, dest], -1)
                column = jnp.where(sub == half * slots + k, row, column)
        put(q + 1, column)
        return 0

    lax.fori_loop(0, n // 2, pair, 0, unroll=2)
    group = sub // hubs
    for k, at in enumerate(pieces):
        arrivals[k].wait()
        part = jnp.dot(select[:, at], feats[at, :], preferred_element_type=F32)
        found[...] = part if k == 0 else found[...] + part
    hub = jnp.zeros((hubs * chunks, LANES), F32)
    for c in range(chunks):
        hub = jnp.where(group == c, found[0 : 2 * slots, c * LANES : (c + 1) * LANES], hub)
    hub = hub.astype(BF16)
    per = LANES // slots
    sent = []
    for b in range(n // per):
        for s in range(per):
            dest = b * per + s
            staged[dest, 0:SUBS, :] = hub
            mine = found[2 * slots + dest * slots : 2 * slots + (dest + 1) * slots, :]
            for c in range(0, chunks, 2):
                both = jnp.concatenate(
                    [mine[:, c * LANES : (c + 1) * LANES], mine[:, (c + 1) * LANES : (c + 2) * LANES]], axis=0
                )
                staged[dest, SUBS + c * slots : SUBS + (c + 2) * slots, :] = both.astype(BF16)
        group_of = pl.ds(b * per, per)
        sent.append(start(staged.at[group_of], out.at[group_of], out_sems.at[b]))
    for copy in sent:
        copy.wait()


def pack_rows(n, send_rows, send_count, hub_rows, features):
    slots, hubs = send_rows.shape[1], hub_rows.shape[0]
    rows, width = features.shape
    packed = (n, (slots + hubs) * width // LANES, LANES)
    return pl.pallas_call(
        functools.partial(pack_kernel, n, slots, hubs),
        out_shape=pltpu.HBM(packed, BF16),
        in_specs=[HBM] * 4,
        out_specs=HBM,
        scratch_shapes=[
            pltpu.SMEM(send_rows.shape, I32),
            pltpu.SMEM(send_count.shape, I32),
            pltpu.SMEM(hub_rows.shape, I32),
            pltpu.VMEM((rows, width), BF16),
            pltpu.VMEM((n * slots + 2 * slots, rows), BF16),
            pltpu.VMEM((n * slots + 2 * slots, width), F32),
            pltpu.VMEM(packed, BF16),
            DMA((3,)),
            DMA((2,)),
            DMA((n * slots // LANES,)),
        ],
        compiler_params=params(16 << 20),
        name="pack_rows",
    )(*in_hbm(send_rows, send_count, hub_rows, features))


def make_plan(tile_rows, tile_cols, blocks, plan, waiting):
    def clear(i, _):
        waiting[i] = NONE
        return 0

    lax.fori_loop(0, 4 * KEYS, clear, 0, unroll=8)
    for kind in range(4):
        plan[COUNTS + kind] = 0

    def add(kind, key, t):
        slot = kind * KEYS + key
        first, count = waiting[slot], plan[COUNTS + kind]
        pair = first != NONE
        plan[kind * LIST + count] = (key << 16) | (first << 8) | t
        plan[COUNTS + kind] = count + pair.astype(I32)
        waiting[slot] = jnp.where(pair, NONE, t)

    def tile(t, _):
        row, col = tile_rows[t], tile_cols[t]
        far = (col >= blocks).astype(I32)
        add(NEAR_FWD + far, row, t)
        add(NEAR_BWD + far, col - blocks * far, t)
        return 0

    lax.fori_loop(0, tile_rows.shape[0], tile, 0)
    for kind in range(4):

        def left(key, count, kind=kind):
            first = waiting[kind * KEYS + key]
            plan[kind * LIST + count] = (key << 16) | (first << 8) | NONE
            return count + (first != NONE).astype(I32)

        count = lax.fori_loop(0, KEYS, left, plan[COUNTS + kind])
        plan[COUNTS + kind] = count
        for u in range(UNROLL):
            plan[kind * LIST + count + u] = (NONE << 8) | NONE


def run_plan(kind, plan, tiles, source_of, source, total, transposed):
    size, last = tiles.shape[1], tiles.shape[0] - 1
    axis = 0 if transposed else 1

    def group(g, _):
        for u in range(UNROLL):
            word = plan[kind * LIST + g * UNROLL + u]
            key, picks = word >> 16, ((word >> 8) & 255, word & 255)
            left, right = [], []
            for pick in picks:
                t = jnp.minimum(pick, last)
                left.append(jnp.where(pick == NONE, jnp.zeros((size, size), BF16), tiles[t]))
                right.append(source[rows_at(source_of(t), size), :])
            total[rows_at(key, size), :] += lax.dot_general(
                jnp.concatenate(left, axis=axis),
                jnp.concatenate(right, axis=0),
                (((axis,), (0,)), ((), ())),
                preferred_element_type=F32,
            )
        return 0

    lax.fori_loop(0, (plan[COUNTS + kind] + UNROLL - 1) // UNROLL, group, 0)


def make_spread(n, slots, hubs, chunks, send_rows, send_count, hub_rows, spread):
    rows = spread.shape[0]
    lane = lax.broadcasted_iota(I32, (SUBS, LANES), 1)
    sub = lax.broadcasted_iota(I32, (SUBS, LANES), 0)

    def put(part, targets):
        def rows_of(b, _):
            hit = jnp.where(targets == sub + b * SUBS, 1.0, 0.0)
            spread[rows_at(b, SUBS), part * LANES : (part + 1) * LANES] = hit.astype(BF16)
            return 0

        lax.fori_loop(0, rows // SUBS, rows_of, 0, unroll=8)

    per = LANES // slots
    for part in range(n * slots // LANES):

        def dest(s, targets, part=part):
            count = send_count[0, part * per + s]
            for k in range(slots):
                row = jnp.where(k < count, send_rows[0, k, part * per + s], -1)
                targets = jnp.where(lane == s * slots + k, row, targets)
            return targets

        put(part, lax.fori_loop(0, per, dest, jnp.full((SUBS, LANES), -1, I32)))
    targets = jnp.full((SUBS, LANES), -1, I32)
    for at in range(2 * hubs * chunks):
        targets = jnp.where(lane == at, hub_rows[at % hubs], targets)
    put(n * slots // LANES, targets)


def near_forward_kernel(
    n, slots, hubs, tile_rows_in, tile_cols_in, send_rows_in, send_count_in, hub_rows_in, tiles, feats_in,
    near_out, plan_out, spread_out,
    tile_rows, tile_cols, send_rows, send_count, hub_rows, feats, total, rounded, spread, plan, waiting, sems,
):
    rows, width = feats.shape
    blocks = rows // tiles.shape[1]
    moves = (
        (tile_rows_in, tile_rows),
        (tile_cols_in, tile_cols),
        (send_rows_in, send_rows),
        (send_count_in, send_count),
        (hub_rows_in, hub_rows),
        (feats_in, feats),
    )
    copies = [start(a, b, sems.at[i]) for i, (a, b) in enumerate(moves)]
    total[...] = jnp.zeros_like(total)
    copies[0].wait()
    copies[1].wait()
    make_plan(tile_rows, tile_cols, blocks, plan, waiting)
    sent = [start(plan, plan_out, sems.at[0])]
    for copy in copies[2:]:
        copy.wait()
    run_plan(NEAR_FWD, plan, tiles, lambda t: jnp.minimum(tile_cols[t], blocks - 1), feats, total, False)
    rounded[...] = total[...].astype(BF16)
    sent.append(start(rounded, near_out, sems.at[1]))
    make_spread(n, slots, hubs, width // LANES, send_rows, send_count, hub_rows, spread)
    sent.append(start(spread, spread_out, sems.at[2]))
    for copy in sent:
        copy.wait()


def near_forward(n, tile_rows, tile_cols, send_rows, send_count, hub_rows, tiles, features):
    rows, width = features.shape
    slots, hubs = send_rows.shape[1], hub_rows.shape[0]
    return pl.pallas_call(
        functools.partial(near_forward_kernel, n, slots, hubs),
        out_shape=(
            pltpu.HBM((rows, width), BF16),
            pltpu.HBM((PLAN,), I32),
            pltpu.HBM((rows, n * slots + LANES), BF16),
        ),
        in_specs=[HBM] * 5 + [VMEM, HBM],
        out_specs=(HBM, HBM, HBM),
        scratch_shapes=[
            pltpu.SMEM(tile_rows.shape, I32),
            pltpu.SMEM(tile_cols.shape, I32),
            pltpu.SMEM(send_rows.shape, I32),
            pltpu.SMEM(send_count.shape, I32),
            pltpu.SMEM(hub_rows.shape, I32),
            pltpu.VMEM((rows, width), BF16),
            pltpu.VMEM((rows, width), F32),
            pltpu.VMEM((rows, width), BF16),
            pltpu.VMEM((rows, n * slots + LANES), BF16),
            pltpu.SMEM((PLAN,), I32),
            pltpu.SMEM((4 * KEYS,), I32),
            DMA((6,)),
        ],
        compiler_params=params(20 << 20),
        cost_estimate=cost(4 << 30, 8 << 20),
        name="near_forward",
    )(
        *in_hbm(tile_rows, tile_cols, send_rows, send_count, hub_rows),
        *in_vmem(tiles),
        *in_hbm(features),
    )


def unpack_slots(n, slots, chunks, packed, into, at):
    def pair(q, _):
        for c in range(0, chunks, 2):
            spot = slice(SUBS + c * slots, SUBS + (c + 2) * slots)
            first = packed[2 * q, spot, :].astype(F32)
            second = packed[2 * q + 1, spot, :].astype(F32)
            for half in range(2):
                part = slice(half * slots, (half + 1) * slots)
                both = jnp.concatenate([first[part], second[part]], axis=0).astype(BF16)
                where = pl.ds(pl.multiple_of(at + q * 2 * slots, 2 * slots), 2 * slots)
                into[where, (c + half) * LANES : (c + half + 1) * LANES] = both
        return 0

    lax.fori_loop(0, n // 2, pair, 0, unroll=4)


def pack_grads(n, slots, hubs, chunks, total, staged):
    def two(q, _):
        both = total[rows_at(q, 2 * hubs), :]
        for u in range(2):
            mine = both[u * hubs : (u + 1) * hubs]
            staged[2 * q + u, 0:SUBS, :] = jnp.concatenate(
                [mine[:, c * LANES : (c + 1) * LANES] for c in range(chunks)], axis=0
            ).astype(BF16)
            halo = total[pl.ds(pl.multiple_of(n * hubs + (2 * q + u) * slots, slots), slots), :]
            for c in range(0, chunks, 2):
                pair = jnp.concatenate(
                    [halo[:, c * LANES : (c + 1) * LANES], halo[:, (c + 1) * LANES : (c + 2) * LANES]], axis=0
                )
                staged[2 * q + u, SUBS + c * slots : SUBS + (c + 2) * slots, :] = pair.astype(BF16)
        return 0

    lax.fori_loop(0, n // 2, two, 0, unroll=2)


def place():
    device = lax.axis_index("dom")
    out = jnp.zeros((), I32)
    for at, bit in enumerate(HALVED):
        out = out | (((device >> bit) & 1) << (len(HALVED) - 1 - at))
    return out


def forward_kernel(
    n, slots, hubs, tile_rows_in, tile_cols_in, plan_in, tiles, received, near_in, weight_in, cot_in,
    output, grad_agg_out, far_out, keep, give,
    tile_rows, tile_cols, plan, table, total, far_total, staged, near, weight, cot, agg, grad_pre, grad_agg, out, sems, near_sems, cot_sems, out_sems, ga_sems,
):
    size = tiles.shape[1]
    rows, width = near.shape
    chunks = width // LANES
    blocks = rows // size
    step = 256
    steps = rows // step
    index = [
        start(a, b, sems.at[i])
        for i, (a, b) in enumerate(((plan_in, plan), (tile_rows_in, tile_rows), (tile_cols_in, tile_cols)))
    ]
    weight_copy = start(weight_in, weight, sems.at[3])
    pieces = [pl.ds(b * step, step) for b in range(steps)]
    arrivals = [
        (start(near_in.at[at], near.at[at], near_sems.at[b]), start(cot_in.at[at], cot.at[at], cot_sems.at[b]))
        for b, at in enumerate(pieces)
    ]
    total[...] = jnp.zeros_like(total)
    far_total[...] = jnp.zeros_like(far_total)

    def four(q, _):
        parts = [received[4 * q + u, 0:SUBS, :].astype(F32) for u in range(4)]
        for c in range(chunks):
            quad = jnp.concatenate([part[c * hubs : (c + 1) * hubs] for part in parts], axis=0)
            table[rows_at(q, SUBS), c * LANES : (c + 1) * LANES] = quad.astype(BF16)
        return 0

    lax.fori_loop(0, n // 4, four, 0, unroll=2)
    unpack_slots(n, slots, chunks, received, table, n * hubs)
    for copy in index:
        copy.wait()
    run_plan(FAR_FWD, plan, tiles, lambda t: jnp.maximum(tile_cols[t] - blocks, 0), table, total, False)
    weight_copy.wait()

    def arrive(blocks_of):
        for pair in arrivals[blocks_of]:
            for copy in pair:
                copy.wait()

    def first(at):
        here = (total[at, :] + near[at, :].astype(F32)).astype(BF16)
        agg[at, :] = here
        return jnp.dot(here, weight[...], preferred_element_type=F32)

    sent = []
    arrive(slice(0, steps // 2))
    pre = first(pieces[0])
    for b, at in enumerate(pieces):
        if b + 1 == steps // 2:
            arrive(slice(steps // 2, steps))
        following = first(pieces[b + 1]) if b + 1 < steps else None
        sig = 0.5 * jnp.tanh(0.5 * pre) + 0.5
        out[at, :] = (pre * sig).astype(BF16)
        gp = (cot[at, :].astype(F32) * sig * (1.0 + pre * (1.0 - sig))).astype(BF16)
        grad_pre[at, :] = gp
        grad_agg[at, :] = lax.dot_general(
            gp, weight[...], (((1,), (1,)), ((), ())), preferred_element_type=F32
        ).astype(BF16)
        sent.append(start(out.at[at], output.at[at], out_sems.at[b]))
        sent.append(start(grad_agg.at[at], grad_agg_out.at[at], ga_sems.at[b]))
        pre = following
    run_plan(FAR_BWD, plan, tiles, lambda t: tile_rows[t], grad_agg, far_total, True)
    pack_grads(n, slots, hubs, chunks, far_total, staged)
    sent.append(start(staged, far_out, sems.at[0]))
    scale = float(rows * n) ** -0.5
    term = total.at[pl.ds(0, width)]
    for c in range(0, width, 256):
        term[c : c + 256, :] = (
            lax.dot_general(
                agg[:, c : c + 256], grad_pre[...], (((0,), (0,)), ((), ())), preferred_element_type=F32
            )
            * scale
        )
    half = 1 << (len(HALVED) - 1)
    unit = width // (2 * half)
    mine = place()
    for b in range(half):
        spot = slice(b * unit, (b + 1) * unit)
        keep[spot, :] = term[rows_at(mine ^ b, unit), :]
        give[spot, :] = term[rows_at(mine ^ (b + half), unit), :].astype(BF16)
    for copy in sent:
        copy.wait()


def forward(n, slots, hubs, tile_rows, tile_cols, plan, tiles, received, near, weight, cotangent):
    rows, width = near.shape
    packed = (n, (slots + hubs) * width // LANES, LANES)
    steps = rows // 256
    return pl.pallas_call(
        functools.partial(forward_kernel, n, slots, hubs),
        out_shape=(
            pltpu.HBM((rows, width), BF16),
            pltpu.HBM((rows, width), BF16),
            pltpu.HBM(packed, BF16),
            pltpu.VMEM((width // 2, width), F32),
            pltpu.VMEM((width // 2, width), BF16),
        ),
        in_specs=[HBM, HBM, HBM, VMEM, VMEM, HBM, HBM, HBM],
        out_specs=(HBM, HBM, HBM, VMEM, VMEM),
        scratch_shapes=[
            pltpu.SMEM(tile_rows.shape, I32),
            pltpu.SMEM(tile_cols.shape, I32),
            pltpu.SMEM((PLAN,), I32),
            pltpu.VMEM((n * (slots + hubs), width), BF16),
            pltpu.VMEM((rows, width), F32),
            pltpu.VMEM((n * (slots + hubs), width), F32),
            pltpu.VMEM(packed, BF16),
            pltpu.VMEM((rows, width), BF16),
            pltpu.VMEM((width, width), BF16),
            pltpu.VMEM((rows, width), BF16),
            pltpu.VMEM((rows, width), BF16),
            pltpu.VMEM((rows, width), BF16),
            pltpu.VMEM((rows, width), BF16),
            pltpu.VMEM((rows, width), BF16),
            DMA((4,)),
            DMA((steps,)),
            DMA((steps,)),
            DMA((steps,)),
            DMA((steps,)),
        ],
        compiler_params=params(28 << 20),
        cost_estimate=cost(8 << 30, 16 << 20),
        name="forward",
    )(*in_hbm(tile_rows, tile_cols, plan), *in_vmem(tiles, received), *in_hbm(near, weight, cotangent))


def near_backward_kernel(
    tile_rows_in, plan_in, tiles_in, grad_agg_in, out, tile_rows, plan, tiles, grad_agg, total, sems
):
    near = tiles_in.at[pl.ds(0, LOC_TILES)]
    moves = ((tile_rows_in, tile_rows), (plan_in, plan), (grad_agg_in, grad_agg), (near, tiles))
    copies = [start(a, b, sems.at[i]) for i, (a, b) in enumerate(moves)]
    total[...] = jnp.zeros_like(total)
    for copy in copies:
        copy.wait()
    run_plan(NEAR_BWD, plan, tiles, lambda t: tile_rows[t], grad_agg, total, True)
    out[...] = total[...].astype(BF16)


def near_backward(tile_rows, plan, tiles, grad_agg):
    return pl.pallas_call(
        near_backward_kernel,
        out_shape=pltpu.VMEM(grad_agg.shape, BF16),
        in_specs=[HBM] * 4,
        out_specs=VMEM,
        scratch_shapes=[
            pltpu.SMEM(tile_rows.shape, I32),
            pltpu.SMEM((PLAN,), I32),
            pltpu.VMEM((LOC_TILES,) + tiles.shape[1:], BF16),
            pltpu.VMEM(grad_agg.shape, BF16),
            pltpu.VMEM(grad_agg.shape, F32),
            DMA((4,)),
        ],
        compiler_params=params(16 << 20),
        cost_estimate=cost(0, 0),
        name="near_backward",
    )(*in_hbm(tile_rows, plan, tiles, grad_agg))


def collect_kernel(
    n, slots, hubs, near, spread_in, returned, out, spread, table, staged, spread_sems, out_sems
):
    rows, width = staged.shape
    chunks = width // LANES
    step = 256
    pieces = [pl.ds(at, step) for at in range(0, rows, step)]
    arrival = start(spread_in, spread, spread_sems.at[0])
    unpack_slots(n, slots, chunks, returned, table, 0)
    hub = lax.fori_loop(
        0, n, lambda s, held: held + returned[s, 0:SUBS, :].astype(F32), jnp.zeros((SUBS, LANES), F32), unroll=8
    )
    group = lax.broadcasted_iota(I32, (SUBS, LANES), 0) // hubs
    base = n * slots
    table[base : base + LANES, :] = jnp.zeros((LANES, width), BF16)
    upper = hub.astype(BF16).astype(F32)
    for at, part in ((0, upper), (SUBS, hub - upper)):
        for c in range(chunks):
            table[base + at : base + at + SUBS, c * LANES : (c + 1) * LANES] = jnp.where(
                group == c, part, 0.0
            ).astype(BF16)
    sent = []
    arrival.wait()
    for b, at in enumerate(pieces):
        more = jnp.dot(spread[at, :], table[...], preferred_element_type=F32)
        staged[at, :] = (near[at, :].astype(F32) + more).astype(BF16)
        sent.append(start(staged.at[at], out.at[at], out_sems.at[b]))
    for copy in sent:
        copy.wait()


def collect(n, slots, hubs, near, spread, returned):
    rows, width = near.shape
    table = n * slots + LANES
    return pl.pallas_call(
        functools.partial(collect_kernel, n, slots, hubs),
        out_shape=pltpu.HBM((rows, width), BF16),
        in_specs=[VMEM, HBM, VMEM],
        out_specs=HBM,
        scratch_shapes=[
            pltpu.VMEM((rows, table), BF16),
            pltpu.VMEM((table, width), BF16),
            pltpu.VMEM((rows, width), BF16),
            DMA((1,)),
            DMA((rows // 256,)),
        ],
        compiler_params=params(16 << 20),
        cost_estimate=cost(32 << 30, 8 << 20),
        name="collect",
    )(*in_vmem(near), *in_hbm(spread), *in_vmem(returned))


def order_kernel(first, second, out):
    half = 1 << (len(HALVED) - 1)
    unit = out.shape[0] // (2 * half)
    mine = place()
    for b in range(half):
        spot = slice(b * unit, (b + 1) * unit)
        out[rows_at(mine ^ b, unit), :] = first[spot, :].astype(F32)
        out[rows_at(mine ^ (b + half), unit), :] = second[spot, :].astype(F32)


def exchange(x, n, mask):
    return lax.ppermute(x, "dom", [(i, i ^ mask) for i in range(n)])


def tie(*arrays):
    return lax.optimization_barrier(arrays)


def all_to_all(x):
    return lax.all_to_all(x, "dom", split_axis=0, concat_axis=0, tiled=True)


def per_device(
    features, weight, cotangent, tile_values, tile_rows, tile_cols, hub_rows, send_rows, send_count
):
    n = lax.axis_size("dom")
    slots, hubs = send_rows.shape[2], hub_rows.shape[0]
    width = features.shape[1]
    send_rows = jnp.swapaxes(send_rows, 1, 2)

    packed = pack_rows(n, send_rows, send_count, hub_rows, features)
    received = all_to_all(packed)
    near, plan, spread = near_forward(
        n, tile_rows, tile_cols, send_rows, send_count, hub_rows, tile_values, features
    )
    output, grad_agg, far, keep, give = forward(
        n, slots, hubs, tile_rows, tile_cols, plan, tile_values, received, near, weight, cotangent
    )
    core, one, other = (1 << bit for bit in HALVED)
    got = exchange(give, n, core)
    quarters = (keep + got.astype(F32)).astype(BF16).reshape(4, keep.shape[0] // 4, width)
    *quarters, far, grad_agg = tie(*(quarters[i] for i in range(4)), far, grad_agg)
    parts = [quarters[0]] + [exchange(quarters[i], n, mask) for i, mask in ((1, other), (2, one), (3, one | other))]
    returned = all_to_all(far)
    a, b, c, d = (part.astype(F32) for part in parts)
    near_grad = near_backward(tile_rows, plan, tile_values, grad_agg)
    held, near_grad = tie(((a + b) + (c + d)).astype(BF16), near_grad)
    parts = [held] + [exchange(held, n, mask) for mask in (8, 16, 24)]
    a, b, c, d = (part.astype(F32) for part in parts)
    held = lax.optimization_barrier(((a + b) + (c + d)).astype(BF16))
    for bit in range(5, n.bit_length() - 1):
        held = (held.astype(F32) + exchange(held, n, 1 << bit).astype(F32)).astype(BF16)
    held, near_grad, returned = tie(held, near_grad, returned)
    parts = [exchange(held, n, mask) for mask in (other, one, one | other)]
    grad_features = collect(n, slots, hubs, near_grad, spread, returned)
    held, grad_features = tie(jnp.concatenate([held] + parts, axis=0), grad_features)
    grad_weight = pl.pallas_call(
        order_kernel,
        out_shape=jax.ShapeDtypeStruct((width, width), F32),
        in_specs=[VMEM, VMEM],
        out_specs=VMEM,
        compiler_params=params(4 << 20),
        name="order",
    )(held, exchange(held, n, core))
    return (output, grad_features, grad_weight)


def solution(mesh):
    placed = (
        P("dom", None),
        P(),
        P("dom", None),
        P("dom", None, None),
        P("dom"),
        P("dom"),
        P("dom"),
        P("dom", None, None),
        P("dom", None),
    )
    return jax.shard_map(
        per_device,
        mesh=mesh,
        in_specs=placed,
        out_specs=(P("dom", None), P("dom", None), P()),
        check_vma=False,
    )
```
